256 devices in a mesh: dp: 4 (over y), seq: 64 (over z, x, core).
Axes of the slice: x: 4, y: 4, z: 8, core: 2. Of those that a mesh axis runs over, the one named last changes fastest.
Arguments:
- query: bfloat16 [4, 16384, 1536], P('dp', 'seq'), may hold values from -6 to 6
- key: bfloat16 [4, 16384, 1536], P('dp', 'seq'), may hold values from -6 to 6
- value: bfloat16 [4, 16384, 1536], P('dp', 'seq'), may hold values from -6 to 6
- segments: int32 [4, 16384], P('dp', 'seq'), may hold values from 0 to 95, never falling along the last dimension, each value on 1 to 256 neighbouring positions
- out_proj: bfloat16 [1536, 1536], replicated, may hold values from -0.15625 to 0.15625
- conv_kernel: bfloat16 [31, 1536], replicated, may hold values from -1 to 1
- cotangent: bfloat16 [4, 16384, 1536], P('dp', 'seq'), may hold values from -6 to 6
Outputs:
- block_out: bfloat16 [4, 16384, 1536], P('dp', 'seq')
- grad_query: bfloat16 [4, 16384, 1536], P('dp', 'seq')
- grad_key: bfloat16 [4, 16384, 1536], P('dp', 'seq')
- grad_value: bfloat16 [4, 16384, 1536], P('dp', 'seq')
- grad_kernel: float32 [31, 1536], replicated
- grad_out_proj: float32 [1536, 1536], P(('dp', 'seq'))
The draws below stay inside these ranges and needn't reach their ends.
Inputs may be any that keep to these rules, and one draw needn't show every extreme that they name: `segments`: along the frames of a data group the utterance number never falls; every utterance holds 1 to 256 frames and one holds exactly 256.
All inputs are finite; a program needn't handle non-finite values.
Results may differ from the reference program's by a relative error of at most 0.02.
Values may be sent and summed in bfloat16 or wider, within the bound.
No kernel may reach another device: no remote copies, remote signals or barrier semaphores. Data moves between devices by JAX's collectives and lax.ppermute only.
A program may use at most 128 MiB of HBM per device.

```python
import math
import jax
import jax.numpy as jnp
import numpy as np
from jax import lax

D = 1536
HEADS = 24
HD = 64
KW = 31
REACH = 15
FR_DEV = 256
FRAMES = 16384
UTTS = 96
ALL_FRAMES = 65536
N_DP = 4
N_SEQ = 64


def drawn_pair(key):
    shape = (N_DP, FRAMES, D)
    query_out = jnp.clip(jax.random.normal(jax.random.fold_in(key, 21), shape, jnp.float32), -4.0, 4.0)
    keys_out = jnp.clip(jax.random.normal(jax.random.fold_in(key, 22), shape, jnp.float32), -4.0, 4.0)
    return (query_out, keys_out)


def draw_query(key, part):
    return drawn_pair(key)[0].astype(jnp.bfloat16)


def draw_key(key, part):
    return drawn_pair(key)[1].astype(jnp.bfloat16)


def level_of(own_key, shape, cuts, low, high):
    loudness, own = 1.0, jax.random.fold_in(own_key, 6)
    for position, shards_of in cuts:
        draws = jnp.exp(jax.random.uniform(jax.random.fold_in(own, position), (shards_of,), jnp.float32, low / len(cuts), high / len(cuts)))
        loudness = loudness * jnp.repeat(draws, shape[position] // shards_of).reshape([-1 if axis == position else 1 for axis in range(len(shape))])
    return loudness


def profile(count, total, reach, lean):
    weights = [(1 << 20) // math.isqrt(grade ** lean) + 1 for grade in range(2, count + 1)]
    surplus, given = total - reach - (count - 1), [1] * (count - 1)
    while surplus > 0:
        free = [i for i in range(count - 1) if given[i] < reach]
        whole, remaining = sum([weights[i] for i in free]), surplus
        for i in free:
            addition = min(reach - given[i], max(1, remaining * weights[i] // whole), surplus)
            given[i] = given[i] + addition
            surplus = surplus - addition
    return np.array([reach] + given)


def ragged_sizes(stream_key, count, total, most, slope):
    if count == 2:
        one = jax.random.randint(stream_key, (), max(1, total - most), min(most, total - 1) + 1)
        return jnp.stack([one, total - one])
    lengths = jnp.asarray(profile(count, total, most, slope), jnp.int32)
    twos = (count - 1) // 2
    donor, taker = lengths[1:1 + 2 * twos:2], lengths[2:2 + 2 * twos:2]
    room = jnp.minimum(donor - 1, most - taker)
    moved = jax.random.randint(jax.random.fold_in(stream_key, 1), (twos,), 0, 1 << 20) % (room + 1)
    lengths = lengths.at[1:1 + 2 * twos:2].set(donor - moved).at[2:2 + 2 * twos:2].set(taker + moved)
    return lengths[jax.random.permutation(jax.random.fold_in(stream_key, 2), count)]


def scatter_about(key, shape, scale, limit, cuts=(), kind=jnp.bfloat16):
    factor_of = level_of(key, shape, cuts, -0.22, 0.18) if cuts else 1.0
    drawn = jax.random.normal(key, shape, jnp.float32) * scale * factor_of
    return jnp.minimum(jnp.maximum(drawn, -limit), limit).astype(kind)


def setup_inputs(seed: int = 0) -> dict:
    key_list = jax.random.split(jax.random.key(seed), 8)
    return {
        "query": draw_query(jax.random.fold_in(key_list[7], 71), 0),
        "key": draw_key(jax.random.fold_in(key_list[7], 71), 0),
        "value": scatter_about(key_list[2], (N_DP, FRAMES, D), 1.0, 6.0, ((0, 4), (1, 64))),
        "segments": jax.vmap(lambda own: jnp.searchsorted(jnp.cumsum(ragged_sizes(own, UTTS, FRAMES, FR_DEV, 1)), jnp.arange(FRAMES), side="right"))(jax.random.split(key_list[3], N_DP)).reshape((N_DP, FRAMES)).astype(jnp.int32),
        "out_proj": scatter_about(key_list[4], (D, D), D ** -0.5, 0.15625),
        "conv_kernel": scatter_about(key_list[5], (KW, D), KW ** -0.5, 1.0),
        "cotangent": scatter_about(key_list[6], (N_DP, FRAMES, D), 1.0, 6.0, ((0, 4), (1, 64))),
    }


def rounded(values):
    return lax.optimization_barrier(values.astype(jnp.bfloat16)).astype(jnp.float32)


def head_scores(queries, keys_block, query_ids, key_ids):
    query_heads = queries.astype(jnp.float32).reshape(queries.shape[0], HEADS, HD)
    key_heads = keys_block.astype(jnp.float32).reshape(keys_block.shape[0], HEADS, HD)
    scores = jnp.einsum("rhe,whe->hrw", query_heads, key_heads) * (HD ** -0.5)
    allowed = query_ids[:, None] == key_ids[None, :]
    return jnp.where(allowed[None], scores, -1e30)


def one_group(query, key, value, group_ids, out_proj, conv_kernel, cotangent):
    frame_ids = group_ids + 1
    key_pad = jnp.pad(key, ((FR_DEV, FR_DEV), (0, 0)))
    value_pad = jnp.pad(value, ((FR_DEV, FR_DEV), (0, 0)))
    ids_pad = jnp.pad(frame_ids, (FR_DEV, FR_DEV))
    starts = jnp.arange(N_SEQ, dtype=jnp.int32) * FR_DEV
    window = 3 * FR_DEV

    def forward_block(start):
        queries = lax.dynamic_slice_in_dim(query, start, FR_DEV, 0)
        keys_block = lax.dynamic_slice_in_dim(key_pad, start, window, 0)
        values_block = lax.dynamic_slice_in_dim(value_pad, start, window, 0)
        scores = head_scores(queries, keys_block, lax.dynamic_slice_in_dim(frame_ids, start, FR_DEV, 0), lax.dynamic_slice_in_dim(ids_pad, start, window, 0))
        highest = jnp.max(scores, axis=2)
        weights = jnp.exp(scores - highest[:, :, None])
        totals = jnp.sum(weights, axis=2)
        probs = rounded(weights / totals[:, :, None])
        context = jnp.einsum("hrw,whe->rhe", probs, values_block.astype(jnp.float32).reshape(window, HEADS, HD))
        return context.reshape(FR_DEV, D), highest, totals

    context, highest, totals = lax.map(forward_block, starts)
    context = context.reshape(FRAMES, D)
    context_b = context.astype(jnp.bfloat16)
    attended = jnp.dot(context_b, out_proj, preferred_element_type=jnp.float32).astype(jnp.bfloat16)
    attended_pad = jnp.pad(attended, ((REACH, REACH), (0, 0))).astype(jnp.float32)
    conv_ids = jnp.pad(frame_ids, (REACH, REACH))
    kernel = conv_kernel.astype(jnp.float32)
    convolved = jnp.zeros((FRAMES, D), jnp.float32)
    for offset in range(KW):
        allowed = (conv_ids[offset:offset + FRAMES] == frame_ids)[:, None]
        convolved = convolved + jnp.where(allowed, kernel[offset] * attended_pad[offset:offset + FRAMES], 0.0)
    gate = jax.nn.sigmoid(convolved)
    block_out = (convolved * gate).astype(jnp.bfloat16)
    conv_grad = (cotangent.astype(jnp.float32) * gate * (1.0 + convolved * (1.0 - gate))).astype(jnp.bfloat16)
    conv_grad_f = conv_grad.astype(jnp.float32)
    conv_grad_pad = jnp.pad(conv_grad_f, ((REACH, REACH), (0, 0)))
    attended_grad = jnp.zeros((FRAMES, D), jnp.float32)
    kernel_rows = []
    for offset in range(KW):
        mirror = 2 * REACH - offset
        mirror_allowed = (conv_ids[mirror:mirror + FRAMES] == frame_ids)[:, None]
        attended_grad = attended_grad + jnp.where(mirror_allowed, kernel[offset] * conv_grad_pad[mirror:mirror + FRAMES], 0.0)
        allowed = (conv_ids[offset:offset + FRAMES] == frame_ids)[:, None]
        kernel_rows.append(jnp.sum(jnp.where(allowed, conv_grad_f * attended_pad[offset:offset + FRAMES], 0.0), axis=0))
    kernel_term = jnp.stack(kernel_rows)
    attended_grad_b = attended_grad.astype(jnp.bfloat16)
    weight_term = lax.dot_general(context_b, attended_grad_b, (((0,), (0,)), ((), ())), preferred_element_type=jnp.float32)
    context_grad = lax.dot_general(attended_grad_b, out_proj, (((1,), (1,)), ((), ())), preferred_element_type=jnp.float32).astype(jnp.bfloat16)
    deltas = jnp.sum((context_grad.astype(jnp.float32) * context).reshape(FRAMES, HEADS, HD), axis=2)

    def backward_block(carry, inputs):
        key_acc, value_acc = carry
        start, highest_block, totals_block = inputs
        queries = lax.dynamic_slice_in_dim(query, start, FR_DEV, 0)
        keys_block = lax.dynamic_slice_in_dim(key_pad, start, window, 0)
        values_block = lax.dynamic_slice_in_dim(value_pad, start, window, 0)
        scores = head_scores(queries, keys_block, lax.dynamic_slice_in_dim(frame_ids, start, FR_DEV, 0), lax.dynamic_slice_in_dim(ids_pad, start, window, 0))
        probs = jnp.exp(scores - highest_block[:, :, None]) / totals_block[:, :, None]
        probs_b = rounded(probs)
        upstream = lax.dynamic_slice_in_dim(context_grad, start, FR_DEV, 0).astype(jnp.float32).reshape(FR_DEV, HEADS, HD)
        value_heads = values_block.astype(jnp.float32).reshape(window, HEADS, HD)
        key_heads = keys_block.astype(jnp.float32).reshape(window, HEADS, HD)
        query_heads = queries.astype(jnp.float32).reshape(FR_DEV, HEADS, HD)
        prob_grads = jnp.einsum("rhe,whe->hrw", upstream, value_heads)
        delta_block = lax.dynamic_slice_in_dim(deltas, start, FR_DEV, 0).T
        score_grad = rounded(probs * (prob_grads - delta_block[:, :, None]) * (HD ** -0.5))
        query_grad = jnp.einsum("hrw,whe->rhe", score_grad, key_heads).reshape(FR_DEV, D)
        key_part = jnp.einsum("hrw,rhe->whe", score_grad, query_heads).reshape(window, D)
        value_part = jnp.einsum("hrw,rhe->whe", probs_b, upstream).reshape(window, D)
        key_acc = lax.dynamic_update_slice_in_dim(key_acc, lax.dynamic_slice_in_dim(key_acc, start, window, 0) + key_part, start, 0)
        value_acc = lax.dynamic_update_slice_in_dim(value_acc, lax.dynamic_slice_in_dim(value_acc, start, window, 0) + value_part, start, 0)
        return (key_acc, value_acc), query_grad

    empty = jnp.zeros((FRAMES + 2 * FR_DEV, D), jnp.float32)
    (key_acc, value_acc), query_grads = lax.scan(backward_block, (empty, empty), (starts, highest, totals))
    grad_query = query_grads.reshape(FRAMES, D).astype(jnp.bfloat16)
    grad_key = key_acc[FR_DEV:FR_DEV + FRAMES].astype(jnp.bfloat16)
    grad_value = value_acc[FR_DEV:FR_DEV + FRAMES].astype(jnp.bfloat16)
    return block_out, grad_query, grad_key, grad_value, kernel_term, weight_term


def reference(query, key, value, segments, out_proj, conv_kernel, cotangent):
    outputs = []
    kernel_total = jnp.zeros((KW, D), jnp.float32)
    weight_total = jnp.zeros((D, D), jnp.float32)
    for group in range(N_DP):
        results = one_group(query[group], key[group], value[group], segments[group], out_proj, conv_kernel, cotangent[group])
        outputs.append(results[:4])
        kernel_total = kernel_total + results[4]
        weight_total = weight_total + results[5]
    scale_out = ALL_FRAMES ** -0.5
    block_out = jnp.stack([entry[0] for entry in outputs])
    grad_query = jnp.stack([entry[1] for entry in outputs])
    grad_key = jnp.stack([entry[2] for entry in outputs])
    grad_value = jnp.stack([entry[3] for entry in outputs])
    return (block_out, grad_query, grad_key, grad_value, kernel_total * scale_out, weight_total * scale_out)
```

```python
import functools

import jax
import jax.numpy as jnp
from jax import lax
from jax.experimental import pallas as pl
from jax.experimental.pallas import tpu as pltpu
from jax.sharding import PartitionSpec as P

HD = 64
KW = 31
ROWS = 256
EDGE = 32
CEDGE = 16
QROWS = ROWS + 2 * EDGE
CROWS = ROWS + 2 * CEDGE
WINDOW = 3 * ROWS
WIDTH = 1536
PARTS = 2
PWIDTH = WIDTH // PARTS
LANES = 256
VMEM = 60 * 1024 * 1024
BF = jnp.bfloat16
F32 = jnp.float32
NT = (((1,), (1,)), ((), ()))
TN = (((0,), (0,)), ((), ()))


def half_masks(scale):
    lane = lax.broadcasted_iota(jnp.int32, (1, 2 * HD), 1)
    return [
        jnp.where((lane < HD) == (half == 0), scale, 0.0).astype(BF) for half in range(2)
    ]


def forward_kernel(
    row_ids, key_ids, q_low, q_own, q_high, k_low, k_own, k_high, v_low, v_own, v_high,
    context_ref, context_b_ref, probs_ref, bias,
):
    @pl.when(pl.program_id(0) == 0)
    def _():
        bias[...] = jnp.where(row_ids[...][:, :1] == key_ids[...], 0.0, -1e30)

    scales = half_masks(HD ** -0.5)
    lane = lax.broadcasted_iota(jnp.int32, (1, 2 * HD), 1) < HD
    for pair in range(q_own.shape[1] // (2 * HD)):
        cols = slice(pair * 2 * HD, (pair + 1) * 2 * HD)
        q = jnp.concatenate([q_low[:, cols], q_own[:, cols], q_high[:, cols]], axis=0)
        k = jnp.concatenate([k_low[:, cols], k_own[:, cols], k_high[:, cols]], axis=0)
        v = jnp.concatenate([v_low[:, cols], v_own[:, cols], v_high[:, cols]], axis=0)
        outs = []
        for half in range(2):
            scores = lax.dot_general(q * scales[half], k, NT, preferred_element_type=F32)
            scores = scores + bias[...]
            highest = jnp.max(scores, axis=1, keepdims=True)
            weights = jnp.exp(scores - highest)
            totals = jnp.sum(weights, axis=1, keepdims=True)
            probs = (weights * (1.0 / totals)).astype(BF)
            probs_ref[2 * pair + half] = probs[EDGE : EDGE + ROWS]
            outs.append(jnp.dot(probs, v, preferred_element_type=F32))
        context = jnp.where(lane, outs[0], outs[1])
        context_ref[:, cols] = context[EDGE : EDGE + ROWS]
        context_b_ref[:, cols] = context.astype(BF)


def attention_forward(row_ids, key_ids, q, k, v, width):
    step = 2 * HD
    heads = step // HD
    column = lambda rows: pl.BlockSpec((rows, step), lambda i: (0, i))
    whole = lambda shape: pl.BlockSpec(shape, lambda i: (0, 0))
    return pl.pallas_call(
        forward_kernel,
        grid=(width // step,),
        out_shape=(
            jax.ShapeDtypeStruct((ROWS, width), F32),
            jax.ShapeDtypeStruct((QROWS, width), BF),
            jax.ShapeDtypeStruct((width // HD, ROWS, WINDOW), BF),
        ),
        in_specs=[whole((QROWS, 128)), whole((1, WINDOW)), column(EDGE), column(ROWS), column(EDGE)]
        + [column(ROWS)] * 6,
        out_specs=(
            column(ROWS),
            column(QROWS),
            pl.BlockSpec((heads, ROWS, WINDOW), lambda i: (i, 0, 0)),
        ),
        scratch_shapes=[pltpu.VMEM((QROWS, WINDOW), F32)],
        compiler_params=pltpu.CompilerParams(vmem_limit_bytes=VMEM),
        cost_estimate=pl.CostEstimate(
            flops=8 * QROWS * WINDOW * width, bytes_accessed=20 << 20, transcendentals=0
        ),
        name="attention_forward",
    )(row_ids, key_ids, *q, *k, *v)


def conv_kernel_body(
    ids_ref, context_ref, weight_ref, taps_ref, cot_ref,
    block_ref, grad_ref, taps_grad_ref, context_grad_ref,
    shifted, cgrad, ids, gated, total, taps_acc,
):
    step = pl.program_id(0)

    @pl.when(step == 0)
    def _():
        ids[0] = ids_ref[...]
        for b in range(1, 8):
            ids[b, : QROWS - 8] = ids_ref[b : b + QROWS - 8, :]
        total[...] = jnp.zeros_like(total)

    shifted[0] = (
        jnp.dot(context_ref[...], weight_ref[...], preferred_element_type=F32).astype(BF).astype(F32)
    )
    for b in range(1, 8):
        shifted[b, : QROWS - 8] = shifted[0, b : b + QROWS - 8, :]
    taps_acc[...] = jnp.zeros_like(taps_acc)
    tiles = [slice(j * 128, (j + 1) * 128) for j in range(LANES // 128)]
    block = 32

    def forward_rows(i, carry):
        o = pl.multiple_of(i * block, block)
        own = ids[0, pl.ds(o + CEDGE, block), :]
        sums = [jnp.zeros((block, 128), F32) for _ in tiles]
        for e in range(1, KW + 1):
            a, b = divmod(e, 8)
            same = ids[b, pl.ds(o + 8 * a, block), :] == own
            for j, tile in enumerate(tiles):
                term = shifted[b, pl.ds(o + 8 * a, block), tile] * taps_ref[e - 1 : e, tile]
                sums[j] = sums[j] + jnp.where(same, term, 0.0)
        for j, tile in enumerate(tiles):
            gate = jax.nn.sigmoid(sums[j])
            gated[pl.ds(o, block), tile] = sums[j] * gate
            grad = cot_ref[pl.ds(o, block), tile].astype(F32) * gate * (1.0 + sums[j] * (1.0 - gate))
            cgrad[0, pl.ds(o, block), tile] = grad.astype(BF).astype(F32)
        return carry

    lax.fori_loop(0, CROWS // block, forward_rows, 0)
    block_ref[...] = gated[CEDGE : CEDGE + ROWS].astype(BF)
    for b in range(1, 8):
        cgrad[b, : CROWS - 8] = cgrad[0, b : b + CROWS - 8, :]

    def backward_rows(i, carry):
        s = pl.multiple_of(i * block, block)
        own = ids[0, pl.ds(s + EDGE, block), :]
        grads = [cgrad[0, pl.ds(s + CEDGE, block), tile] for tile in tiles]
        sums = [jnp.zeros((block, 128), F32) for _ in tiles]
        for e in range(1, KW + 1):
            a, b = divmod(e, 8)
            same = ids[b, pl.ds(s + CEDGE + 8 * a, block), :] == own
            for j, tile in enumerate(tiles):
                term = cgrad[b, pl.ds(s + 8 * a, block), tile] * taps_ref[KW - e : KW - e + 1, tile]
                sums[j] = sums[j] + jnp.where(same, term, 0.0)
                pair = grads[j] * shifted[b, pl.ds(s + CEDGE + 8 * a, block), tile]
                pair = jnp.where(same, pair, 0.0)
                taps_acc[e - 1, :, tile] += jnp.sum(pair.reshape(block // 8, 8, 128), axis=0)
        for j, tile in enumerate(tiles):
            grad_ref[pl.ds(s, block), tile] = sums[j].astype(BF)
        return carry

    lax.fori_loop(0, ROWS // block, backward_rows, 0)
    taps_grad_ref[...] = jnp.sum(taps_acc[...], axis=1)
    total[...] += lax.dot_general(grad_ref[...], weight_ref[...], NT, preferred_element_type=F32)

    @pl.when(step == pl.num_programs(0) - 1)
    def _():
        context_grad_ref[...] = total[...].astype(BF)


def conv_chain(row_ids, context_b, out_proj, taps, cot_wide):
    column = lambda rows: pl.BlockSpec((rows, LANES), lambda i: (0, i))
    whole = lambda shape: pl.BlockSpec(shape, lambda i: (0, 0))
    return pl.pallas_call(
        conv_kernel_body,
        grid=(WIDTH // LANES,),
        out_shape=(
            jax.ShapeDtypeStruct((ROWS, WIDTH), BF),
            jax.ShapeDtypeStruct((ROWS, WIDTH), BF),
            jax.ShapeDtypeStruct((KW + 1, WIDTH), F32),
            jax.ShapeDtypeStruct((ROWS, WIDTH), BF),
        ),
        in_specs=[
            whole((QROWS, 128)), whole((QROWS, WIDTH)), column(WIDTH), column(KW + 1), column(CROWS),
        ],
        out_specs=(column(ROWS), column(ROWS), column(KW + 1), whole((ROWS, WIDTH))),
        scratch_shapes=[
            pltpu.VMEM((8, QROWS, LANES), F32),
            pltpu.VMEM((8, CROWS, LANES), F32),
            pltpu.VMEM((8, QROWS, 128), F32),
            pltpu.VMEM((CROWS, LANES), F32),
            pltpu.VMEM((ROWS, WIDTH), F32),
            pltpu.VMEM((KW + 1, 8, LANES), F32),
        ],
        compiler_params=pltpu.CompilerParams(vmem_limit_bytes=VMEM),
        cost_estimate=pl.CostEstimate(flops=20 << 30, bytes_accessed=10 << 20, transcendentals=0),
        name="conv_chain",
    )(row_ids, context_b, out_proj, taps, cot_wide)


def backward_kernel(
    q_own, k_low, k_own, k_high, v_low, v_own, v_high, upstream, context, probs_ref,
    dq_ref, dk_low, dk_own, dk_high, dv_low, dv_own, dv_high,
):
    plain = half_masks(1.0)
    scales = half_masks(HD ** -0.5)
    lane = lax.broadcasted_iota(jnp.int32, (1, 2 * HD), 1) < HD
    for pair in range(q_own.shape[1] // (2 * HD)):
        cols = slice(pair * 2 * HD, (pair + 1) * 2 * HD)
        k = jnp.concatenate([k_low[:, cols], k_own[:, cols], k_high[:, cols]], axis=0)
        v = jnp.concatenate([v_low[:, cols], v_own[:, cols], v_high[:, cols]], axis=0)
        q = q_own[:, cols]
        up = upstream[:, cols]
        products = up.astype(F32) * context[:, cols]
        q_turned = q.astype(F32).T.astype(BF)
        up_turned = up.astype(F32).T.astype(BF)
        dqs, dks, dvs = [], [], []
        for half in range(2):
            rows = slice(half * HD, (half + 1) * HD)
            delta = jnp.sum(
                jnp.where(lane == (half == 0), products, 0.0), axis=1, keepdims=True
            ) * HD ** -0.5
            grads = lax.dot_general(up * scales[half], v, NT, preferred_element_type=F32)
            probs = probs_ref[2 * pair + half]
            score_grad = (probs.astype(F32) * (grads - delta)).astype(BF)
            dqs.append(jnp.dot(score_grad, k, preferred_element_type=F32))
            dks.append(jnp.dot(q_turned[rows], score_grad, preferred_element_type=F32))
            dvs.append(jnp.dot(up_turned[rows], probs, preferred_element_type=F32))
        dq_ref[:, cols] = jnp.where(lane, dqs[0], dqs[1]).astype(BF)
        for parts, low, own, high in ((dks, dk_low, dk_own, dk_high), (dvs, dv_low, dv_own, dv_high)):
            whole = jnp.concatenate(parts, axis=0).T
            low[:, cols] = whole[:ROWS].astype(BF)
            own[:, cols] = whole[ROWS : 2 * ROWS]
            high[:, cols] = whole[2 * ROWS :].astype(BF)


def attention_backward(q, k, v, upstream, context, probs):
    width = upstream.shape[1]
    step = 2 * HD
    heads = step // HD
    column = pl.BlockSpec((ROWS, step), lambda i: (0, i))
    bf = jax.ShapeDtypeStruct((ROWS, width), BF)
    own = jax.ShapeDtypeStruct((ROWS, width), F32)
    return pl.pallas_call(
        backward_kernel,
        grid=(width // step,),
        out_shape=(bf, bf, own, bf, bf, own, bf),
        in_specs=[column] * 9 + [pl.BlockSpec((heads, ROWS, WINDOW), lambda i: (i, 0, 0))],
        out_specs=(column,) * 7,
        compiler_params=pltpu.CompilerParams(vmem_limit_bytes=VMEM),
        cost_estimate=pl.CostEstimate(
            flops=10 * ROWS * WINDOW * width, bytes_accessed=20 << 20, transcendentals=0
        ),
        name="attention_backward",
    )(q, *k, *v, upstream, context, probs)


def product_kernel(mine, theirs, grad_mine, grad_theirs, taps_mine, taps_theirs, *outs):
    taps = (taps_mine[...] + taps_theirs[...]).astype(BF)
    count = outs[0].shape[0] - 8
    for part in range(PARTS):
        cols = slice(part * PWIDTH, (part + 1) * PWIDTH)
        for block in range(4):
            rows = slice(block * count, (block + 1) * count)
            out = outs[4 * part + block]
            out[:count] = (
                jnp.dot(mine[rows], grad_mine[:, cols], preferred_element_type=F32)
                + jnp.dot(theirs[rows], grad_theirs[:, cols], preferred_element_type=F32)
            ).astype(BF)
            out[count:] = taps[8 * block : 8 * block + 8, cols]


def product_blocks(mine, theirs, grad_mine, grad_theirs, taps_mine, taps_theirs):
    shape = jax.ShapeDtypeStruct((mine.shape[0] // 4 + 8, PWIDTH), BF)
    return pl.pallas_call(
        product_kernel,
        out_shape=(shape,) * (4 * PARTS),
        compiler_params=pltpu.CompilerParams(vmem_limit_bytes=VMEM),
        cost_estimate=pl.CostEstimate(flops=2 << 30, bytes_accessed=8 << 20, transcendentals=0),
        name="product_blocks",
    )(mine, theirs, grad_mine, grad_theirs, taps_mine, taps_theirs)


def combine_kernel(sources, pieces, count, *refs):
    ins, outs = refs[:sources], refs[sources : sources + pieces]
    held = refs[-1]
    total = ins[0][...].astype(F32)
    for ref in ins[1:]:
        total = total + ref[...].astype(F32)
    held[...] = total
    rows = count // pieces
    for piece in range(pieces):
        out = outs[piece]
        if out.shape[0] > rows + 8:
            out[...] = jnp.zeros_like(out)
        out[:rows] = held[piece * rows : (piece + 1) * rows].astype(out.dtype)
        out[rows : rows + 8] = held[count : count + 8].astype(out.dtype)


def combine(blocks, count, pieces, out_rows, dtype):
    shape = jax.ShapeDtypeStruct((out_rows, blocks[0].shape[1]), dtype)
    return pl.pallas_call(
        functools.partial(combine_kernel, len(blocks), pieces, count),
        out_shape=(shape,) * pieces,
        scratch_shapes=[pltpu.VMEM(blocks[0].shape, F32)],
        compiler_params=pltpu.CompilerParams(vmem_limit_bytes=VMEM),
        name="combine",
    )(*blocks)


def seq_pairs(shift):
    pairs = []
    for source in range(64):
        z, x, c = source // 8, (source // 2) % 4, source % 2
        tz, tx, tc = shift(z, x, c)
        pairs.append((source, ((tz % 8) * 4 + tx % 4) * 2 + tc))
    return pairs


SWAP = seq_pairs(lambda z, x, c: (z, x, 1 - c))
UP = [(i, i + 1) for i in range(63)]
DOWN = [(i + 1, i) for i in range(63)]


def per_device(query, key, value, segments, out_proj, conv_kernel, cotangent):
    q, k, v, cot = query[0], key[0], value[0], cotangent[0]
    dp = lax.axis_index("dp")
    seq = lax.axis_index("seq")
    z, x, c = seq // 8, (seq // 2) % 4, seq % 2
    own_ids = segments[0] + 1

    id_row = lax.pad(own_ids.astype(BF)[None], jnp.zeros((), BF), ((0, 15, 0), (0, WIDTH - ROWS, 0)))
    up_small = jnp.concatenate([q[ROWS - EDGE :], cot[ROWS - CEDGE :], id_row], axis=0)
    down_small = jnp.concatenate([q[:EDGE], cot[:CEDGE], id_row], axis=0)
    low_small = lax.ppermute(up_small, "seq", UP)
    high_small = lax.ppermute(down_small, "seq", DOWN)
    k_low = lax.ppermute(k, "seq", UP)
    k_high = lax.ppermute(k, "seq", DOWN)
    v_low = lax.ppermute(v, "seq", UP)
    v_high = lax.ppermute(v, "seq", DOWN)
    ids = jnp.concatenate(
        [
            low_small[EDGE + CEDGE, :ROWS].astype(F32),
            own_ids.astype(F32),
            high_small[EDGE + CEDGE, :ROWS].astype(F32),
        ]
    )
    row_ids = jnp.broadcast_to(ids[ROWS - EDGE : 2 * ROWS + EDGE, None], (QROWS, 128))
    key_ids = ids[None]
    cot_wide = jnp.concatenate(
        [low_small[EDGE : EDGE + CEDGE], cot, high_small[EDGE : EDGE + CEDGE]], axis=0
    )
    taps = lax.pad(conv_kernel.astype(F32), jnp.zeros((), F32), ((0, 1, 0), (0, 0, 0)))

    keys = (k_low, k, k_high)
    values = (v_low, v, v_high)
    context, context_b, probs = attention_forward(
        row_ids, key_ids, (low_small[:EDGE], q, high_small[:EDGE]), keys, values, WIDTH
    )

    place = lax.broadcasted_iota(jnp.int32, (WIDTH, 1), 0)
    tc = (place // 768) ^ c
    ty = (place // 192 + dp) % 4
    tx = (place // 48 + x) % 4
    tz = (place // 6 + z) % 8
    target = 6 * (64 * ty + 8 * tz + 2 * tx + tc) + place % 6
    chosen = (target == lax.broadcasted_iota(jnp.int32, (1, WIDTH), 1)).astype(BF)
    own_context = context_b[EDGE : EDGE + ROWS]
    half = WIDTH // 2
    sent = lax.dot_general(chosen[half:], own_context, NT, preferred_element_type=F32).astype(BF)
    mine = lax.dot_general(chosen[:half], own_context, NT, preferred_element_type=F32).astype(BF)
    theirs = lax.ppermute(sent, "seq", SWAP)

    block_out, attended_grad, taps_grad, context_grad = conv_chain(
        row_ids, context_b, out_proj, taps, cot_wide
    )
    taps_grad = jnp.roll(taps_grad, -8 * dp, axis=0)
    grad_theirs = lax.ppermute(attended_grad, "seq", SWAP)
    taps_theirs = lax.ppermute(taps_grad, "seq", SWAP)
    blocks = product_blocks(mine, theirs, attended_grad, grad_theirs, taps_grad, taps_theirs)

    weight_parts, taps_parts = [], []
    scale_out = (4 * 64 * ROWS) ** (-0.5)
    for part in range(PARTS):
        held = blocks[4 * part : 4 * part + 4]
        got = [
            lax.ppermute(held[n], "dp", [(i, (i + n) % 4) for i in range(4)]) for n in (1, 2, 3)
        ]
        held = combine([held[0]] + got, 192, 4, 56, BF)
        got = [
            lax.ppermute(held[n], "seq", seq_pairs(lambda z, x, c: (z, x + n, c))) for n in (1, 2, 3)
        ]
        held = combine([held[0]] + got, 48, 8, 16, BF)
        got = [
            lax.ppermute(held[n], "seq", seq_pairs(lambda z, x, c: (z + n, x, c)))
            for n in range(1, 8)
        ]
        (last,) = combine([held[0]] + got, 6, 1, 16, F32)
        weight_parts.append(last[:6])
        taps_parts.append(last[6:14])
    grad_out_proj = jnp.concatenate(weight_parts, axis=1) * scale_out
    taps_rows = jnp.concatenate(taps_parts, axis=1) * scale_out
    others = [
        lax.ppermute(taps_rows, "dp", [(i, (i - n) % 4) for i in range(4)]) for n in (1, 2, 3)
    ]
    ring = jnp.concatenate([taps_rows] + others, axis=0)
    grad_kernel = jnp.roll(ring, 8 * dp, axis=0)[:KW]

    dq, dk_low, dk_own, dk_high, dv_low, dv_own, dv_high = attention_backward(
        q, keys, values, context_grad, context, probs
    )
    dk_later = lax.ppermute(dk_low, "seq", DOWN)
    dk_earlier = lax.ppermute(dk_high, "seq", UP)
    dv_later = lax.ppermute(dv_low, "seq", DOWN)
    dv_earlier = lax.ppermute(dv_high, "seq", UP)
    dk = (dk_own + dk_later.astype(F32) + dk_earlier.astype(F32)).astype(BF)
    dv = (dv_own + dv_later.astype(F32) + dv_earlier.astype(F32)).astype(BF)
    return (block_out[None], dq[None], dk[None], dv[None], grad_kernel, grad_out_proj)


def solution(mesh):
    in_specs = (
        P("dp", "seq", None),
        P("dp", "seq", None),
        P("dp", "seq", None),
        P("dp", "seq"),
        P(),
        P(),
        P("dp", "seq", None),
    )
    out_specs = (
        P("dp", "seq", None),
        P("dp", "seq", None),
        P("dp", "seq", None),
        P("dp", "seq", None),
        P(),
        P(("dp", "seq"), None),
    )
    return jax.shard_map(
        per_device, mesh=mesh, in_specs=in_specs, out_specs=out_specs, check_vma=False
    )
```

```python
import functools

import jax
import jax.numpy as jnp
from jax import lax
from jax.experimental import pallas as pl
from jax.experimental.pallas import tpu as pltpu
from jax.sharding import PartitionSpec as P

HD = 64
KW = 31
ROWS = 256
EDGE = 32
CEDGE = 16
QROWS = ROWS + 2 * EDGE
CROWS = ROWS + 2 * CEDGE
WINDOW = 3 * ROWS
WIDTH = 1536
CALLS = ((0, 3), (3, 2), (5, 1))
CHUNKS = 2
CWIDTH = WIDTH // CHUNKS
LANES = 256
VMEM = 60 * 1024 * 1024
BF = jnp.bfloat16
F32 = jnp.float32
NT = (((1,), (1,)), ((), ()))
TN = (((0,), (0,)), ((), ()))


def half_masks(scale):
    lane = lax.broadcasted_iota(jnp.int32, (1, 2 * HD), 1)
    return [
        jnp.where((lane < HD) == (half == 0), scale, 0.0).astype(BF) for half in range(2)
    ]


def forward_kernel(
    row_ids, key_ids, q_low, q_own, q_high, k_low, k_own, k_high, v_low, v_own, v_high,
    context_ref, context_b_ref, probs_ref, bias,
):
    @pl.when(pl.program_id(0) == 0)
    def _():
        bias[...] = jnp.where(row_ids[...][:, :1] == key_ids[...], 0.0, -1e30)

    scales = half_masks(HD ** -0.5)
    lane = lax.broadcasted_iota(jnp.int32, (1, 2 * HD), 1) < HD
    for pair in range(q_own.shape[1] // (2 * HD)):
        cols = slice(pair * 2 * HD, (pair + 1) * 2 * HD)
        q = jnp.concatenate([q_low[:, cols], q_own[:, cols], q_high[:, cols]], axis=0)
        k = jnp.concatenate([k_low[:, cols], k_own[:, cols], k_high[:, cols]], axis=0)
        v = jnp.concatenate([v_low[:, cols], v_own[:, cols], v_high[:, cols]], axis=0)
        outs = []
        for half in range(2):
            scores = lax.dot_general(q * scales[half], k, NT, preferred_element_type=F32)
            scores = scores + bias[...]
            highest = jnp.max(scores, axis=1, keepdims=True)
            weights = jnp.exp(scores - highest)
            totals = jnp.sum(weights, axis=1, keepdims=True)
            probs = (weights * (1.0 / totals)).astype(BF)
            probs_ref[2 * pair + half] = probs[EDGE : EDGE + ROWS]
            outs.append(jnp.dot(probs, v, preferred_element_type=F32))
        context = jnp.where(lane, outs[0], outs[1])
        context_ref[:, cols] = context[EDGE : EDGE + ROWS]
        context_b_ref[:, cols] = context.astype(BF)


def attention_forward(row_ids, key_ids, q, k, v, low, high, chunk):
    step = 2 * HD
    heads = step // HD
    first = chunk * (CWIDTH // step)
    column = lambda rows: pl.BlockSpec((rows, step), lambda i: (0, i))
    offset = lambda rows, at=0: pl.BlockSpec((rows, step), lambda i: (at, i + first))
    second = pl.BlockSpec((ROWS, step), lambda i: (1, i))
    edge = pl.BlockSpec((EDGE, step), lambda i: (2 * ROWS // EDGE, i))
    whole = lambda shape: pl.BlockSpec(shape, lambda i: (0, 0))
    return pl.pallas_call(
        forward_kernel,
        grid=(CWIDTH // step,),
        out_shape=(
            jax.ShapeDtypeStruct((ROWS, CWIDTH), F32),
            jax.ShapeDtypeStruct((QROWS, CWIDTH), BF),
            jax.ShapeDtypeStruct((CWIDTH // HD, ROWS, WINDOW), BF),
        ),
        in_specs=[
            whole((QROWS, 128)), whole((1, WINDOW)), edge, offset(ROWS), edge,
            column(ROWS), offset(ROWS), column(ROWS), second, offset(ROWS), second,
        ],
        out_specs=(
            column(ROWS),
            column(QROWS),
            pl.BlockSpec((heads, ROWS, WINDOW), lambda i: (i, 0, 0)),
        ),
        scratch_shapes=[pltpu.VMEM((QROWS, WINDOW), F32)],
        compiler_params=pltpu.CompilerParams(vmem_limit_bytes=VMEM),
        cost_estimate=pl.CostEstimate(
            flops=12 << 30, bytes_accessed=10 << 20, transcendentals=0
        ),
        name="attention_forward",
    )(row_ids, key_ids, low, q, high, low, k, high, low, v, high)


def conv_kernel_body(*refs):
    ids_ref = refs[0]
    contexts = refs[1 : 1 + CHUNKS]
    weight_ref, taps_ref, cot_low, cot_own, cot_high = refs[1 + CHUNKS : 6 + CHUNKS]
    rest = refs[6 + CHUNKS :]
    block_ref, grad_ref, shifted, cgrad, ids, gated, taps_acc, cot_ref = rest[-8:]
    step = pl.program_id(0)

    @pl.when(step == 0)
    def _():
        ids[0] = ids_ref[...]
        for b in range(1, 8):
            ids[b, : QROWS - 8] = ids_ref[b : b + QROWS - 8, :]

    cot_ref[:CEDGE] = cot_low[...].astype(F32)
    cot_ref[CEDGE : CEDGE + ROWS] = cot_own[...].astype(F32)
    cot_ref[CEDGE + ROWS :] = cot_high[...].astype(F32)
    attended = jnp.zeros((QROWS, LANES), F32)
    for n, context_ref in enumerate(contexts):
        attended = attended + jnp.dot(
            context_ref[...], weight_ref[n * CWIDTH : (n + 1) * CWIDTH], preferred_element_type=F32
        )
    shifted[0] = attended.astype(BF).astype(F32)
    for b in range(1, 8):
        shifted[b, : QROWS - 8] = shifted[0, b : b + QROWS - 8, :]
    taps_acc[...] = jnp.zeros_like(taps_acc)
    tiles = [slice(j * 128, (j + 1) * 128) for j in range(LANES // 128)]
    block = 32

    def forward_rows(i, carry):
        o = pl.multiple_of(i * block, block)
        own = ids[0, pl.ds(o + CEDGE, block), :]
        sums = [jnp.zeros((block, 128), F32) for _ in tiles]
        for e in range(1, KW + 1):
            a, b = divmod(e, 8)
            same = ids[b, pl.ds(o + 8 * a, block), :] == own
            for j, tile in enumerate(tiles):
                term = shifted[b, pl.ds(o + 8 * a, block), tile] * taps_ref[e - 1 : e, tile]
                sums[j] = sums[j] + jnp.where(same, term, 0.0)
        for j, tile in enumerate(tiles):
            gate = jax.nn.sigmoid(sums[j])
            gated[pl.ds(o, block), tile] = sums[j] * gate
            grad = cot_ref[pl.ds(o, block), tile] * gate * (1.0 + sums[j] * (1.0 - gate))
            cgrad[0, pl.ds(o, block), tile] = grad.astype(BF).astype(F32)
        return carry

    lax.fori_loop(0, CROWS // block, forward_rows, 0)
    block_ref[...] = gated[CEDGE : CEDGE + ROWS].astype(BF)
    for b in range(1, 8):
        cgrad[b, : CROWS - 8] = cgrad[0, b : b + CROWS - 8, :]

    def backward_rows(i, carry):
        s = pl.multiple_of(i * block, block)
        own = ids[0, pl.ds(s + EDGE, block), :]
        grads = [cgrad[0, pl.ds(s + CEDGE, block), tile] for tile in tiles]
        sums = [jnp.zeros((block, 128), F32) for _ in tiles]
        for e in range(1, KW + 1):
            a, b = divmod(e, 8)
            same = ids[b, pl.ds(s + CEDGE + 8 * a, block), :] == own
            for j, tile in enumerate(tiles):
                term = cgrad[b, pl.ds(s + 8 * a, block), tile] * taps_ref[KW - e : KW - e + 1, tile]
                sums[j] = sums[j] + jnp.where(same, term, 0.0)
                pair = grads[j] * shifted[b, pl.ds(s + CEDGE + 8 * a, block), tile]
                pair = jnp.where(same, pair, 0.0)
                taps_acc[e - 1, :, tile] += jnp.sum(pair.reshape(block // 8, 8, 128), axis=0)
        for j, tile in enumerate(tiles):
            grad_ref[pl.ds(s, block), tile] = sums[j].astype(BF)
        return carry

    lax.fori_loop(0, ROWS // block, backward_rows, 0)
    grad_ref[ROWS:] = jnp.sum(taps_acc[...], axis=1).astype(BF)


def conv_chain(row_ids, contexts, out_proj, taps, lows, cot, highs, block_out, after, call):
    begin, steps = CALLS[call]
    first = call == 0
    width = steps * LANES
    column = lambda rows: pl.BlockSpec((rows, LANES), lambda i: (0, i))
    offset = lambda rows, at=0: pl.BlockSpec((rows, LANES), lambda i: (at, i + begin))
    whole = lambda shape: pl.BlockSpec(shape, lambda i: (0, 0))
    anywhere = pl.BlockSpec(memory_space=pl.ANY)
    chunk = begin * LANES // CWIDTH
    local = begin - chunk * (CWIDTH // LANES)
    edge = pl.BlockSpec((CEDGE, LANES), lambda i: ((2 * ROWS + EDGE) // CEDGE, i + local))
    carried = after if first else [block_out] + after
    return pl.pallas_call(
        conv_kernel_body,
        grid=(steps,),
        out_shape=(
            jax.ShapeDtypeStruct((ROWS, WIDTH), BF),
            jax.ShapeDtypeStruct((ROWS + KW + 1, width), BF),
        ),
        in_specs=[whole((QROWS, 128))]
        + [whole((QROWS, CWIDTH))] * CHUNKS
        + [
            offset(WIDTH), offset(KW + 1),
            edge, offset(ROWS), edge,
        ]
        + [anywhere] * len(carried),
        out_specs=(offset(ROWS), column(ROWS + KW + 1)),
        scratch_shapes=[
            pltpu.VMEM((8, QROWS, LANES), F32),
            pltpu.VMEM((8, CROWS, LANES), F32),
            pltpu.VMEM((8, QROWS, 128), F32),
            pltpu.VMEM((CROWS, LANES), F32),
            pltpu.VMEM((KW + 1, 8, LANES), F32),
            pltpu.VMEM((CROWS, LANES), F32),
        ],
        input_output_aliases={} if first else {6 + CHUNKS: 0},
        compiler_params=pltpu.CompilerParams(vmem_limit_bytes=VMEM),
        cost_estimate=pl.CostEstimate(
            flops=steps * (5 << 30), bytes_accessed=10 << 20, transcendentals=0
        ),
        name="conv_chain",
    )(row_ids, *contexts, out_proj, taps, lows[chunk], cot, highs[chunk], *carried)


def context_grad_kernel(weight_ref, *refs):
    grads, out = refs[: len(CALLS)], refs[-1]
    total = jnp.zeros(out.shape[::-1], F32)
    for (begin, steps), grad in zip(CALLS, grads):
        cols = slice(begin * LANES, (begin + steps) * LANES)
        total = total + lax.dot_general(
            weight_ref[:, cols], grad[:ROWS], NT, preferred_element_type=F32
        )
    out[...] = total.T.astype(BF)


def context_gradient(out_proj, grads, after):
    step = 512
    return pl.pallas_call(
        context_grad_kernel,
        grid=(WIDTH // step,),
        out_shape=jax.ShapeDtypeStruct((ROWS, WIDTH), BF),
        in_specs=[pl.BlockSpec((step, WIDTH), lambda i: (i, 0))]
        + [pl.BlockSpec(grad.shape, lambda i: (0, 0)) for grad in grads]
        + [pl.BlockSpec(memory_space=pl.ANY)] * len(after),
        out_specs=pl.BlockSpec((ROWS, step), lambda i: (0, i)),
        compiler_params=pltpu.CompilerParams(vmem_limit_bytes=VMEM),
        cost_estimate=pl.CostEstimate(flops=3 << 30, bytes_accessed=8 << 20, transcendentals=0),
        name="context_gradient",
    )(out_proj, *grads, *after)


def backward_kernel(
    q_own, k_low, k_own, k_high, v_low, v_own, v_high, upstream, context, probs_ref, *rest,
):
    dq_ref, low_ref, dk_own, dv_own, high_ref = rest[-5:]
    plain = half_masks(1.0)
    scales = half_masks(HD ** -0.5)
    lane = lax.broadcasted_iota(jnp.int32, (1, 2 * HD), 1) < HD
    for pair in range(q_own.shape[1] // (2 * HD)):
        cols = slice(pair * 2 * HD, (pair + 1) * 2 * HD)
        k = jnp.concatenate([k_low[:, cols], k_own[:, cols], k_high[:, cols]], axis=0)
        v = jnp.concatenate([v_low[:, cols], v_own[:, cols], v_high[:, cols]], axis=0)
        q = q_own[:, cols]
        up = upstream[:, cols]
        products = up.astype(F32) * context[:, cols]
        q_turned = q.astype(F32).T.astype(BF)
        up_turned = up.astype(F32).T.astype(BF)
        dqs, dks, dvs = [], [], []
        for half in range(2):
            rows = slice(half * HD, (half + 1) * HD)
            delta = jnp.sum(
                jnp.where(lane == (half == 0), products, 0.0), axis=1, keepdims=True
            ) * HD ** -0.5
            grads = lax.dot_general(up * scales[half], v, NT, preferred_element_type=F32)
            probs = probs_ref[2 * pair + half]
            score_grad = (probs.astype(F32) * (grads - delta)).astype(BF)
            dqs.append(jnp.dot(score_grad, k, preferred_element_type=F32))
            dks.append(jnp.dot(q_turned[rows], score_grad, preferred_element_type=F32))
            dvs.append(jnp.dot(up_turned[rows], probs, preferred_element_type=F32))
        dq_ref[:, cols] = jnp.where(lane, dqs[0], dqs[1]).astype(BF)
        for n, (parts, own) in enumerate(((dks, dk_own), (dvs, dv_own))):
            whole = jnp.concatenate(parts, axis=0).T
            low_ref[n * ROWS : (n + 1) * ROWS, cols] = whole[:ROWS].astype(BF)
            own[:, cols] = whole[ROWS : 2 * ROWS]
            high_ref[n * ROWS : (n + 1) * ROWS, cols] = whole[2 * ROWS :].astype(BF)


def attention_backward(q, k, v, low, high, upstream, context, probs, previous, after, chunk):
    step = 2 * HD
    heads = step // HD
    first = chunk * (CWIDTH // step)
    column = lambda rows: pl.BlockSpec((rows, step), lambda i: (0, i))
    offset = lambda rows: pl.BlockSpec((rows, step), lambda i: (0, i + first))
    second = pl.BlockSpec((ROWS, step), lambda i: (1, i))
    own = jax.ShapeDtypeStruct((ROWS, WIDTH), F32)
    both = jax.ShapeDtypeStruct((2 * ROWS, WIDTH), BF)
    carried = list(previous) + after
    return pl.pallas_call(
        backward_kernel,
        grid=(CWIDTH // step,),
        out_shape=(jax.ShapeDtypeStruct((ROWS, WIDTH), BF), both, own, own, both),
        in_specs=[
            offset(ROWS), column(ROWS), offset(ROWS), column(ROWS), second, offset(ROWS), second,
            offset(ROWS), column(ROWS),
            pl.BlockSpec((heads, ROWS, WINDOW), lambda i: (i, 0, 0)),
        ]
        + [pl.BlockSpec(memory_space=pl.ANY)] * len(carried),
        out_specs=(
            offset(ROWS), offset(2 * ROWS), offset(ROWS), offset(ROWS), offset(2 * ROWS),
        ),
        input_output_aliases={10 + n: n for n in range(len(previous))},
        compiler_params=pltpu.CompilerParams(vmem_limit_bytes=VMEM),
        cost_estimate=pl.CostEstimate(
            flops=10 << 30, bytes_accessed=10 << 20, transcendentals=0
        ),
        name="attention_backward",
    )(q, low, k, high, low, v, high, upstream, context, probs, *carried)


def order_kernel(place_ref, *refs):
    contexts, outs = refs[:CHUNKS], refs[CHUNKS:]
    dp, z, x, c = (place_ref[n] for n in range(4))
    span = WIDTH // 4
    row = lax.broadcasted_iota(jnp.int32, (span, 1), 0)
    quarter = row // 96
    tc = lax.rem(quarter + c, 2)
    tl = lax.rem(quarter // 2 + z, 2)
    tx = lax.rem(lax.rem(row, 96) // 24 + x, 4)
    th = lax.rem(lax.rem(row, 24) // 6 + z // 2, 4)
    target = 48 * (2 * th + tl) + 12 * tx + 6 * tc + lax.rem(row, 6)
    chosen = jnp.where(
        target == lax.broadcasted_iota(jnp.int32, (1, span), 1), 1.0, 0.0
    ).astype(BF)
    turned = []
    for ref in contexts:
        for n in range(CWIDTH // span):
            part = ref[EDGE : EDGE + ROWS, n * span : (n + 1) * span]
            turned.append(lax.dot_general(chosen, part, NT, preferred_element_type=F32).astype(BF))
    for n in range(4):
        at = pl.ds(pl.multiple_of(96 * lax.rem(n - dp + 4, 4), 32), 96)
        for index, out in enumerate(outs):
            out[at] = turned[n][96 * index : 96 * (index + 1)]


def order_context(place, contexts):
    shape = jax.ShapeDtypeStruct((WIDTH // 4, ROWS), BF)
    vmem = pl.BlockSpec(memory_space=pltpu.VMEM)
    return pl.pallas_call(
        order_kernel,
        out_shape=(shape,) * 4,
        in_specs=[pl.BlockSpec(memory_space=pltpu.SMEM)] + [vmem] * CHUNKS,
        out_specs=(vmem,) * 4,
        compiler_params=pltpu.CompilerParams(vmem_limit_bytes=VMEM),
        name="order_context",
    )(place, *contexts)


def product_kernel(place_ref, *refs):
    contexts, grads, outs = refs[:4], refs[4:-4], refs[-4:]
    at = pl.ds(pl.multiple_of(ROWS + 16 * place_ref[3], 16), 16)
    context = jnp.concatenate([ref[...] for ref in contexts], axis=1)
    for call, (begin, steps) in enumerate(CALLS):
        cols = slice(begin * LANES, (begin + steps) * LANES)
        group = grads[4 * call : 4 * call + 4]
        taps = sum(grad[at].astype(F32) for grad in group).astype(BF)
        grad = jnp.concatenate([ref[:ROWS] for ref in group], axis=0)
        product = jnp.dot(context, grad, preferred_element_type=F32).astype(BF)
        for block in range(4):
            outs[block][:96, cols] = product[block * 96 : (block + 1) * 96]
            outs[block][96:, cols] = taps


def product_blocks(place, contexts, grads):
    shape = jax.ShapeDtypeStruct((112, WIDTH), BF)
    vmem = pl.BlockSpec(memory_space=pltpu.VMEM)
    return pl.pallas_call(
        product_kernel,
        out_shape=(shape,) * 4,
        in_specs=[pl.BlockSpec(memory_space=pltpu.SMEM)] + [vmem] * (4 + len(grads)),
        out_specs=(vmem,) * 4,
        compiler_params=pltpu.CompilerParams(vmem_limit_bytes=VMEM),
        cost_estimate=pl.CostEstimate(flops=3 << 30, bytes_accessed=8 << 20, transcendentals=0),
        name="product_blocks",
    )(place, *contexts, *grads)


def combine_kernel(parts, sources, pieces, count, scale, *refs):
    ins, outs = refs[: parts * sources], refs[-1 - pieces : -1]
    held = refs[-1]
    start = 0
    for part in range(parts):
        group = ins[part * sources : (part + 1) * sources]
        total = group[0][...].astype(F32)
        for ref in group[1:]:
            total = total + ref[...].astype(F32)
        held[:, start : start + group[0].shape[1]] = total * scale
        start = start + group[0].shape[1]
    rows = count // pieces
    for piece in range(pieces):
        out = outs[piece]
        if out.shape[0] > rows + 16:
            out[...] = jnp.zeros_like(out)
        out[:rows] = held[piece * rows : (piece + 1) * rows].astype(out.dtype)
        out[rows : rows + 16] = held[count : count + 16].astype(out.dtype)


def combine(parts, count, pieces, out_rows, after):
    shape = jax.ShapeDtypeStruct((out_rows, WIDTH), BF)
    blocks = [block for part in parts for block in part]
    vmem = pl.BlockSpec(memory_space=pltpu.VMEM)
    return pl.pallas_call(
        functools.partial(combine_kernel, len(parts), len(parts[0]), pieces, count, 1.0),
        out_shape=(shape,) * pieces,
        in_specs=[vmem] * len(blocks) + [pl.BlockSpec(memory_space=pl.ANY)] * len(after),
        out_specs=(vmem,) * pieces,
        scratch_shapes=[pltpu.VMEM((blocks[0].shape[0], WIDTH), F32)],
        compiler_params=pltpu.CompilerParams(vmem_limit_bytes=VMEM),
        cost_estimate=pl.CostEstimate(flops=0, bytes_accessed=1024, transcendentals=0),
        name="combine",
    )(*blocks, *after)


def last_kernel(scale, *refs):
    ins, (weight_out, taps_out, held) = refs[:-3], refs[-3:]
    total = ins[0][...].astype(F32)
    for ref in ins[1:]:
        total = total + ref[...].astype(F32)
    held[...] = total * scale
    weight_out[...] = held[:6]
    taps_out[...] = held[6:22]


def last_combine(blocks, scale):
    return pl.pallas_call(
        functools.partial(last_kernel, scale),
        out_shape=(
            jax.ShapeDtypeStruct((6, WIDTH), F32),
            jax.ShapeDtypeStruct((16, WIDTH), F32),
        ),
        scratch_shapes=[pltpu.VMEM(blocks[0].shape, F32)],
        name="last_combine",
    )(*blocks)


def join_kernel(place_ref, mine, theirs, out, held):
    c = place_ref[3]
    held[pl.ds(pl.multiple_of(16 * c, 16), 16)] = mine[...]
    held[pl.ds(pl.multiple_of(16 * (1 - c), 16), 16)] = theirs[...]
    out[...] = held[:KW]


def join_taps(place, mine, theirs):
    vmem = pl.BlockSpec(memory_space=pltpu.VMEM)
    return pl.pallas_call(
        join_kernel,
        out_shape=jax.ShapeDtypeStruct((KW, WIDTH), F32),
        in_specs=[pl.BlockSpec(memory_space=pltpu.SMEM), vmem, vmem],
        out_specs=vmem,
        scratch_shapes=[pltpu.VMEM((KW + 1, WIDTH), F32)],
        name="join_taps",
    )(place, mine, theirs)


def finish_kernel(*refs):
    dk, dv, later, earlier = refs[:4]
    for own, out, rows in ((dk, refs[-2], slice(0, ROWS)), (dv, refs[-1], slice(ROWS, 2 * ROWS))):
        total = own[...] + later[rows].astype(F32) + earlier[rows].astype(F32)
        out[...] = total.astype(BF)


def finish(operands):
    shape = jax.ShapeDtypeStruct((ROWS, WIDTH), BF)
    column = lambda rows: pl.BlockSpec((rows, 512), lambda i: (0, i))
    return pl.pallas_call(
        finish_kernel,
        grid=(WIDTH // 512,),
        out_shape=(shape, shape),
        in_specs=[column(ROWS), column(ROWS), column(2 * ROWS), column(2 * ROWS)],
        out_specs=(column(ROWS), column(ROWS)),
        compiler_params=pltpu.CompilerParams(vmem_limit_bytes=VMEM),
        cost_estimate=pl.CostEstimate(flops=0, bytes_accessed=1024, transcendentals=0),
        name="finish",
    )(*operands)


def seq_pairs(shift):
    pairs = []
    for source in range(64):
        z, x, c = source // 8, (source // 2) % 4, source % 2
        tz, tx, tc = shift(z, x, c)
        pairs.append((source, ((tz % 8) * 4 + tx % 4) * 2 + tc))
    return pairs


SWAP = seq_pairs(lambda z, x, c: (z, x, 1 - c))
PAIR = seq_pairs(lambda z, x, c: (z ^ 1, x, c))
BOTH = seq_pairs(lambda z, x, c: (z ^ 1, x, 1 - c))
UP = [(i, i + 1) for i in range(63)]
DOWN = [(i + 1, i) for i in range(63)]


def per_device(query, key, value, segments, out_proj, conv_kernel, cotangent):
    q, k, v, cot = query[0], key[0], value[0], cotangent[0]
    dp = lax.axis_index("dp")
    seq = lax.axis_index("seq")
    place = jnp.stack([dp, seq // 8, (seq // 2) % 4, seq % 2]).astype(jnp.int32)
    own_ids = segments[0] + 1

    id_row = lax.pad(
        own_ids.astype(BF)[None], jnp.zeros((), BF), ((0, 15, 0), (0, CWIDTH - ROWS, 0))
    )
    lows, highs = [], []
    for chunk in range(CHUNKS):
        cols = slice(chunk * CWIDTH, (chunk + 1) * CWIDTH)
        sent_up = [k[:, cols], v[:, cols], q[ROWS - EDGE :, cols], cot[ROWS - CEDGE :, cols], id_row]
        sent_down = [k[:, cols], v[:, cols], q[:EDGE, cols], cot[:CEDGE, cols], id_row]
        lows.append(lax.ppermute(jnp.concatenate(sent_up, axis=0), "seq", UP))
        highs.append(lax.ppermute(jnp.concatenate(sent_down, axis=0), "seq", DOWN))
    id_at = 2 * ROWS + EDGE + CEDGE
    ids = jnp.concatenate(
        [
            lows[0][id_at, :ROWS].astype(F32),
            own_ids.astype(F32),
            highs[0][id_at, :ROWS].astype(F32),
        ]
    )
    row_ids = jnp.broadcast_to(ids[ROWS - EDGE : 2 * ROWS + EDGE, None], (QROWS, 128))
    key_ids = ids[None]
    taps = lax.pad(conv_kernel.astype(F32), jnp.zeros((), F32), ((0, 1, 0), (0, 0, 0)))

    attended = [
        attention_forward(
            row_ids, key_ids, q, k, v, lows[chunk], highs[chunk], chunk
        )
        for chunk in range(CHUNKS)
    ]
    contexts = [entry[1] for entry in attended]
    ordered = order_context(place, contexts)
    ordered = [ordered[0]] + [
        lax.ppermute(part, "seq", pairs) for part, pairs in zip(ordered[1:], (SWAP, PAIR, BOTH))
    ]

    block_out, after = None, []
    grads, gathered = [], []
    relayed = None
    for call in range(len(CALLS)):
        block_out, grad = conv_chain(
            row_ids, contexts, out_proj, taps, lows, cot, highs, block_out, after, call
        )
        grads.append(grad)
        across = lax.ppermute(grad, "seq", PAIR)
        if call == 0:
            diagonal = lax.ppermute(across, "seq", SWAP)
        elif call == 1:
            relayed, diagonal = across, None
        else:
            diagonal = lax.ppermute(grad, "seq", BOTH)
            relayed, _ = lax.optimization_barrier((relayed, grad))
            gathered[7] = lax.ppermute(relayed, "seq", SWAP)
        group = [grad, lax.ppermute(grad, "seq", SWAP), across, diagonal]
        after = ordered[1:] if call == 0 else gathered[1:3]
        gathered += group
    context_grad = context_gradient(out_proj, grads, [gathered[3]])
    blocks = product_blocks(place, ordered, gathered)
    got = [lax.ppermute(blocks[n], "dp", [(i, (i + n) % 4) for i in range(4)]) for n in (1, 2, 3)]

    results, after = (), [blocks[0]]
    for chunk in range(CHUNKS):
        results = attention_backward(
            q, k, v, lows[chunk], highs[chunk], context_grad, attended[chunk][0],
            attended[chunk][2], results, after, chunk,
        )
        if chunk == 0:
            held = combine([[blocks[0]] + got], 96, 4, 40, [results[2]])
            after = [held[0]]
            got = [
                lax.ppermute(held[n], "seq", seq_pairs(lambda z, x, c: (z, x + n, c)))
                for n in (1, 2, 3)
            ]
    dq, low, dk, dv, high = results
    low, high, *got = lax.optimization_barrier((low, high, *got))
    later, earlier = lax.ppermute(low, "seq", DOWN), lax.ppermute(high, "seq", UP)
    held = combine([[held[0]] + got], 24, 4, 24, [dk])
    got = [
        lax.ppermute(held[n], "seq", seq_pairs(lambda z, x, c: (z + 2 * n, x, c))) for n in (1, 2, 3)
    ]
    scale_out = (4 * 64 * ROWS) ** (-0.5)
    grad_out_proj, taps_rows = last_combine([held[0]] + got, scale_out)
    grad_kernel = join_taps(place, taps_rows, lax.ppermute(taps_rows, "seq", SWAP))
    dk, dv = finish([dk, dv, later, earlier])
    return (block_out[None], dq[None], dk[None], dv[None], grad_kernel, grad_out_proj)


def solution(mesh):
    in_specs = (
        P("dp", "seq", None),
        P("dp", "seq", None),
        P("dp", "seq", None),
        P("dp", "seq"),
        P(),
        P(),
        P("dp", "seq", None),
    )
    out_specs = (
        P("dp", "seq", None),
        P("dp", "seq", None),
        P("dp", "seq", None),
        P("dp", "seq", None),
        P(),
        P(("dp", "seq"), None),
    )
    return jax.shard_map(
        per_device, mesh=mesh, in_specs=in_specs, out_specs=out_specs, check_vma=False
    )
```

```python
import functools

import jax
import jax.numpy as jnp
from jax import lax
from jax.experimental import pallas as pl
from jax.experimental.pallas import tpu as pltpu
from jax.sharding import PartitionSpec as P

HD = 64
KW = 31
ROWS = 256
EDGE = 32
CEDGE = 16
QROWS = ROWS + 2 * EDGE
CROWS = ROWS + 2 * CEDGE
WINDOW = 3 * ROWS
WIDTH = 1536
CALLS = ((0, 3), (3, 2), (5, 1))
CHUNKS = 2
CWIDTH = WIDTH // CHUNKS
LANES = 256
VMEM = 60 * 1024 * 1024
BF = jnp.bfloat16
F32 = jnp.float32
NT = (((1,), (1,)), ((), ()))
TN = (((0,), (0,)), ((), ()))


def half_masks(scale):
    lane = lax.broadcasted_iota(jnp.int32, (1, 2 * HD), 1)
    return [
        jnp.where((lane < HD) == (half == 0), scale, 0.0).astype(BF) for half in range(2)
    ]


def forward_kernel(
    ids_low, ids_own, ids_high, q_low, q_own, q_high, k_low, k_own, k_high, v_low, v_own, v_high,
    context_ref, context_b_ref, probs_ref, row_ids_ref, bias, turned,
):
    @pl.when(pl.program_id(0) == 0)
    def _():
        key_ids = jnp.concatenate(
            [ids_low[...].astype(F32)[:1], ids_own[...], ids_high[...].astype(F32)[:1]], axis=1
        )
        turned[...] = jnp.broadcast_to(key_ids, (128, WINDOW)).T
        row_ids = turned[ROWS - EDGE : 2 * ROWS + EDGE]
        row_ids_ref[...] = row_ids
        bias[...] = jnp.where(row_ids[:, :1] == key_ids, 0.0, -1e30)

    scales = half_masks(HD ** -0.5)
    lane = lax.broadcasted_iota(jnp.int32, (1, 2 * HD), 1) < HD
    for pair in range(q_own.shape[1] // (2 * HD)):
        cols = slice(pair * 2 * HD, (pair + 1) * 2 * HD)
        q = jnp.concatenate([q_low[:, cols], q_own[:, cols], q_high[:, cols]], axis=0)
        k = jnp.concatenate([k_low[:, cols], k_own[:, cols], k_high[:, cols]], axis=0)
        v = jnp.concatenate([v_low[:, cols], v_own[:, cols], v_high[:, cols]], axis=0)
        outs = []
        for half in range(2):
            scores = lax.dot_general(q * scales[half], k, NT, preferred_element_type=F32)
            scores = scores + bias[...]
            highest = jnp.max(scores, axis=1, keepdims=True)
            weights = jnp.exp(scores - highest)
            totals = jnp.sum(weights, axis=1, keepdims=True)
            probs = (weights * (1.0 / totals)).astype(BF)
            probs_ref[2 * pair + half] = probs[EDGE : EDGE + ROWS]
            outs.append(jnp.dot(probs, v, preferred_element_type=F32))
        context = jnp.where(lane, outs[0], outs[1])
        context_ref[:, cols] = context[EDGE : EDGE + ROWS]
        context_b_ref[:, cols] = context.astype(BF)


def attention_forward(own_ids, q, k, v, low, high, chunk):
    step = 4 * HD
    heads = step // HD
    first = chunk * (CWIDTH // step)
    column = lambda rows: pl.BlockSpec((rows, step), lambda i: (0, i))
    offset = lambda rows, at=0: pl.BlockSpec((rows, step), lambda i: (at, i + first))
    second = pl.BlockSpec((ROWS, step), lambda i: (1, i))
    edge = pl.BlockSpec((EDGE, step), lambda i: (2 * ROWS // EDGE, i))
    whole = lambda shape: pl.BlockSpec(shape, lambda i: (0, 0))
    id_block = pl.BlockSpec((16, ROWS), lambda i: ((2 * ROWS + EDGE + CEDGE) // 16, 0))
    return pl.pallas_call(
        forward_kernel,
        grid=(CWIDTH // step,),
        out_shape=(
            jax.ShapeDtypeStruct((ROWS, CWIDTH), F32),
            jax.ShapeDtypeStruct((QROWS, CWIDTH), BF),
            jax.ShapeDtypeStruct((CWIDTH // HD, ROWS, WINDOW), BF),
            jax.ShapeDtypeStruct((QROWS, 128), F32),
        ),
        in_specs=[
            id_block, whole((1, ROWS)), id_block, edge, offset(ROWS), edge,
            column(ROWS), offset(ROWS), column(ROWS), second, offset(ROWS), second,
        ],
        out_specs=(
            column(ROWS),
            column(QROWS),
            pl.BlockSpec((heads, ROWS, WINDOW), lambda i: (i, 0, 0)),
            whole((QROWS, 128)),
        ),
        scratch_shapes=[pltpu.VMEM((QROWS, WINDOW), F32), pltpu.VMEM((WINDOW, 128), F32)],
        compiler_params=pltpu.CompilerParams(vmem_limit_bytes=VMEM),
        cost_estimate=pl.CostEstimate(
            flops=12 << 30, bytes_accessed=10 << 20, transcendentals=0
        ),
        name="attention_forward",
    )(low, own_ids, high, low, q, high, low, k, high, low, v, high)


def conv_kernel_body(*refs):
    ids_ref = refs[0]
    contexts = refs[1 : 1 + CHUNKS]
    weight_ref, taps_ref, cot_low, cot_own, cot_high = refs[1 + CHUNKS : 6 + CHUNKS]
    rest = refs[6 + CHUNKS :]
    block_ref, grad_ref, shifted, cgrad, ids, gated, taps_acc, cot_ref = rest[-8:]
    step = pl.program_id(0)

    @pl.when(step == 0)
    def _():
        ids[0] = ids_ref[...]
        for b in range(1, 8):
            ids[b, : QROWS - 8] = ids_ref[b : b + QROWS - 8, :]

    cot_ref[:CEDGE] = cot_low[...].astype(F32)
    cot_ref[CEDGE : CEDGE + ROWS] = cot_own[...].astype(F32)
    cot_ref[CEDGE + ROWS :] = cot_high[...].astype(F32)
    attended = jnp.zeros((QROWS, LANES), F32)
    for n, context_ref in enumerate(contexts):
        attended = attended + jnp.dot(
            context_ref[...], weight_ref[n * CWIDTH : (n + 1) * CWIDTH], preferred_element_type=F32
        )
    shifted[0] = attended.astype(BF).astype(F32)
    for b in range(1, 8):
        shifted[b, : QROWS - 8] = shifted[0, b : b + QROWS - 8, :]
    taps_acc[...] = jnp.zeros_like(taps_acc)
    tiles = [slice(j * 128, (j + 1) * 128) for j in range(LANES // 128)]
    block = 32

    def forward_rows(i, carry):
        o = pl.multiple_of(i * block, block)
        own = ids[0, pl.ds(o + CEDGE, block), :]
        sums = [jnp.zeros((block, 128), F32) for _ in tiles]
        for e in range(1, KW + 1):
            a, b = divmod(e, 8)
            same = ids[b, pl.ds(o + 8 * a, block), :] == own
            for j, tile in enumerate(tiles):
                term = shifted[b, pl.ds(o + 8 * a, block), tile] * taps_ref[e - 1 : e, tile]
                sums[j] = sums[j] + jnp.where(same, term, 0.0)
        for j, tile in enumerate(tiles):
            gate = jax.nn.sigmoid(sums[j])
            gated[pl.ds(o, block), tile] = sums[j] * gate
            grad = cot_ref[pl.ds(o, block), tile] * gate * (1.0 + sums[j] * (1.0 - gate))
            cgrad[0, pl.ds(o, block), tile] = grad.astype(BF).astype(F32)
        return carry

    lax.fori_loop(0, CROWS // block, forward_rows, 0)
    block_ref[...] = gated[CEDGE : CEDGE + ROWS].astype(BF)
    for b in range(1, 8):
        cgrad[b, : CROWS - 8] = cgrad[0, b : b + CROWS - 8, :]

    def backward_rows(i, carry):
        s = pl.multiple_of(i * block, block)
        own = ids[0, pl.ds(s + EDGE, block), :]
        grads = [cgrad[0, pl.ds(s + CEDGE, block), tile] for tile in tiles]
        sums = [jnp.zeros((block, 128), F32) for _ in tiles]
        for e in range(1, KW + 1):
            a, b = divmod(e, 8)
            same = ids[b, pl.ds(s + CEDGE + 8 * a, block), :] == own
            for j, tile in enumerate(tiles):
                term = cgrad[b, pl.ds(s + 8 * a, block), tile] * taps_ref[KW - e : KW - e + 1, tile]
                sums[j] = sums[j] + jnp.where(same, term, 0.0)
                pair = grads[j] * shifted[b, pl.ds(s + CEDGE + 8 * a, block), tile]
                pair = jnp.where(same, pair, 0.0)
                taps_acc[e - 1, :, tile] += jnp.sum(pair.reshape(block // 8, 8, 128), axis=0)
        for j, tile in enumerate(tiles):
            grad_ref[pl.ds(s, block), tile] = sums[j].astype(BF)
        return carry

    lax.fori_loop(0, ROWS // block, backward_rows, 0)
    grad_ref[ROWS:] = jnp.sum(taps_acc[...], axis=1).astype(BF)


def conv_chain(row_ids, contexts, out_proj, taps, lows, cot, highs, block_out, after, call):
    begin, steps = CALLS[call]
    first = call == 0
    width = steps * LANES
    column = lambda rows: pl.BlockSpec((rows, LANES), lambda i: (0, i))
    offset = lambda rows, at=0: pl.BlockSpec((rows, LANES), lambda i: (at, i + begin))
    whole = lambda shape: pl.BlockSpec(shape, lambda i: (0, 0))
    anywhere = pl.BlockSpec(memory_space=pl.ANY)
    chunk = begin * LANES // CWIDTH
    local = begin - chunk * (CWIDTH // LANES)
    edge = pl.BlockSpec((CEDGE, LANES), lambda i: ((2 * ROWS + EDGE) // CEDGE, i + local))
    carried = after if first else [block_out] + after
    return pl.pallas_call(
        conv_kernel_body,
        grid=(steps,),
        out_shape=(
            jax.ShapeDtypeStruct((ROWS, WIDTH), BF),
            jax.ShapeDtypeStruct((ROWS + KW + 1, width), BF),
        ),
        in_specs=[whole((QROWS, 128))]
        + [whole((QROWS, CWIDTH))] * CHUNKS
        + [
            offset(WIDTH), offset(KW + 1),
            edge, offset(ROWS), edge,
        ]
        + [anywhere] * len(carried),
        out_specs=(offset(ROWS), column(ROWS + KW + 1)),
        scratch_shapes=[
            pltpu.VMEM((8, QROWS, LANES), F32),
            pltpu.VMEM((8, CROWS, LANES), F32),
            pltpu.VMEM((8, QROWS, 128), F32),
            pltpu.VMEM((CROWS, LANES), F32),
            pltpu.VMEM((KW + 1, 8, LANES), F32),
            pltpu.VMEM((CROWS, LANES), F32),
        ],
        input_output_aliases={} if first else {6 + CHUNKS: 0},
        compiler_params=pltpu.CompilerParams(vmem_limit_bytes=VMEM),
        cost_estimate=pl.CostEstimate(
            flops=steps * (5 << 30), bytes_accessed=10 << 20, transcendentals=0
        ),
        name="conv_chain",
    )(row_ids, *contexts, out_proj, taps, lows[chunk], cot, highs[chunk], *carried)


def context_grad_kernel(weight_ref, *refs):
    grads, out = refs[: len(CALLS)], refs[-1]
    total = jnp.zeros(out.shape[::-1], F32)
    for (begin, steps), grad in zip(CALLS, grads):
        cols = slice(begin * LANES, (begin + steps) * LANES)
        total = total + lax.dot_general(
            weight_ref[:, cols], grad[:ROWS], NT, preferred_element_type=F32
        )
    out[...] = total.T.astype(BF)


def context_gradient(out_proj, grads, after):
    step = 768
    return pl.pallas_call(
        context_grad_kernel,
        grid=(WIDTH // step,),
        out_shape=jax.ShapeDtypeStruct((ROWS, WIDTH), BF),
        in_specs=[pl.BlockSpec((step, WIDTH), lambda i: (i, 0))]
        + [pl.BlockSpec(grad.shape, lambda i: (0, 0)) for grad in grads]
        + [pl.BlockSpec(memory_space=pl.ANY)] * len(after),
        out_specs=pl.BlockSpec((ROWS, step), lambda i: (0, i)),
        compiler_params=pltpu.CompilerParams(vmem_limit_bytes=VMEM),
        cost_estimate=pl.CostEstimate(flops=3 << 30, bytes_accessed=8 << 20, transcendentals=0),
        name="context_gradient",
    )(out_proj, *grads, *after)


def backward_kernel(
    q_own, k_low, k_own, k_high, v_low, v_own, v_high, upstream, context, probs_ref, *rest,
):
    dq_ref, low_ref, dk_own, dv_own, high_ref = rest[-5:]
    plain = half_masks(1.0)
    scales = half_masks(HD ** -0.5)
    lane = lax.broadcasted_iota(jnp.int32, (1, 2 * HD), 1) < HD
    for pair in range(q_own.shape[1] // (2 * HD)):
        cols = slice(pair * 2 * HD, (pair + 1) * 2 * HD)
        k = jnp.concatenate([k_low[:, cols], k_own[:, cols], k_high[:, cols]], axis=0)
        v = jnp.concatenate([v_low[:, cols], v_own[:, cols], v_high[:, cols]], axis=0)
        q = q_own[:, cols]
        up = upstream[:, cols]
        products = up.astype(F32) * context[:, cols]
        q_turned = q.astype(F32).T.astype(BF)
        up_turned = up.astype(F32).T.astype(BF)
        dqs, dks, dvs = [], [], []
        for half in range(2):
            rows = slice(half * HD, (half + 1) * HD)
            delta = jnp.sum(
                jnp.where(lane == (half == 0), products, 0.0), axis=1, keepdims=True
            ) * HD ** -0.5
            grads = lax.dot_general(up * scales[half], v, NT, preferred_element_type=F32)
            probs = probs_ref[2 * pair + half]
            score_grad = (probs.astype(F32) * (grads - delta)).astype(BF)
            dqs.append(jnp.dot(score_grad, k, preferred_element_type=F32))
            dks.append(jnp.dot(q_turned[rows], score_grad, preferred_element_type=F32))
            dvs.append(jnp.dot(up_turned[rows], probs, preferred_element_type=F32))
        dq_ref[:, cols] = jnp.where(lane, dqs[0], dqs[1]).astype(BF)
        for n, (parts, own) in enumerate(((dks, dk_own), (dvs, dv_own))):
            whole = jnp.concatenate(parts, axis=0).T
            low_ref[n * ROWS : (n + 1) * ROWS, cols] = whole[:ROWS].astype(BF)
            own[:, cols] = whole[ROWS : 2 * ROWS]
            high_ref[n * ROWS : (n + 1) * ROWS, cols] = whole[2 * ROWS :].astype(BF)


def attention_backward(q, k, v, low, high, upstream, context, probs, previous, after, chunk, piece):
    step = 4 * HD
    heads = step // HD
    inner, count = piece
    first = chunk * (CWIDTH // step) + inner
    column = lambda rows: pl.BlockSpec((rows, step), lambda i: (0, i + inner))
    offset = lambda rows: pl.BlockSpec((rows, step), lambda i: (0, i + first))
    second = pl.BlockSpec((ROWS, step), lambda i: (1, i + inner))
    own = jax.ShapeDtypeStruct((ROWS, WIDTH), F32)
    both = jax.ShapeDtypeStruct((2 * ROWS, WIDTH), BF)
    carried = list(previous) + after
    return pl.pallas_call(
        backward_kernel,
        grid=(count,),
        out_shape=(jax.ShapeDtypeStruct((ROWS, WIDTH), BF), both, own, own, both),
        in_specs=[
            offset(ROWS), column(ROWS), offset(ROWS), column(ROWS), second, offset(ROWS), second,
            offset(ROWS), column(ROWS),
            pl.BlockSpec((heads, ROWS, WINDOW), lambda i: (i + inner, 0, 0)),
        ]
        + [pl.BlockSpec(memory_space=pl.ANY)] * len(carried),
        out_specs=(
            offset(ROWS), offset(2 * ROWS), offset(ROWS), offset(ROWS), offset(2 * ROWS),
        ),
        input_output_aliases={10 + n: n for n in range(len(previous))},
        compiler_params=pltpu.CompilerParams(vmem_limit_bytes=VMEM),
        cost_estimate=pl.CostEstimate(
            flops=count * (3 << 30), bytes_accessed=10 << 20, transcendentals=0
        ),
        name="attention_backward",
    )(q, low, k, high, low, v, high, upstream, context, probs, *carried)


def order_kernel(place_ref, *refs):
    contexts, outs = refs[:CHUNKS], refs[CHUNKS:]
    dp, z, x, c = (place_ref[n] for n in range(4))
    span = WIDTH // 4
    row = lax.broadcasted_iota(jnp.int32, (span, 1), 0)
    quarter = row // 96
    tc = lax.rem(quarter + c, 2)
    tl = lax.rem(quarter // 2 + z, 2)
    tx = lax.rem(lax.rem(row, 96) // 24 + x, 4)
    th = lax.rem(lax.rem(row, 24) // 6 + z // 2, 4)
    target = 48 * (2 * th + tl) + 12 * tx + 6 * tc + lax.rem(row, 6)
    chosen = jnp.where(
        target == lax.broadcasted_iota(jnp.int32, (1, span), 1), 1.0, 0.0
    ).astype(BF)
    turned = []
    for ref in contexts:
        for n in range(CWIDTH // span):
            part = ref[EDGE : EDGE + ROWS, n * span : (n + 1) * span]
            turned.append(lax.dot_general(chosen, part, NT, preferred_element_type=F32).astype(BF))
    for n in range(4):
        at = pl.ds(pl.multiple_of(96 * lax.rem(n - dp + 4, 4), 32), 96)
        for index, out in enumerate(outs):
            out[at] = turned[n][96 * index : 96 * (index + 1)]


def order_context(place, contexts):
    shape = jax.ShapeDtypeStruct((WIDTH // 4, ROWS), BF)
    vmem = pl.BlockSpec(memory_space=pltpu.VMEM)
    return pl.pallas_call(
        order_kernel,
        out_shape=(shape,) * 4,
        in_specs=[pl.BlockSpec(memory_space=pltpu.SMEM)] + [vmem] * CHUNKS,
        out_specs=(vmem,) * 4,
        compiler_params=pltpu.CompilerParams(vmem_limit_bytes=VMEM),
        name="order_context",
    )(place, *contexts)


def product_kernel(place_ref, *refs):
    contexts, grads, outs = refs[:4], refs[4:-5], refs[-4:]
    at = pl.ds(pl.multiple_of(ROWS + 16 * place_ref[3], 16), 16)
    context = jnp.concatenate([ref[...] for ref in contexts], axis=1)
    for call, (begin, steps) in enumerate(CALLS):
        cols = slice(begin * LANES, (begin + steps) * LANES)
        group = grads[4 * call : 4 * call + 4]
        taps = sum(grad[at].astype(F32) for grad in group).astype(BF)
        grad = jnp.concatenate([ref[:ROWS] for ref in group], axis=0)
        product = jnp.dot(context, grad, preferred_element_type=F32).astype(BF)
        for block in range(4):
            outs[block][:96, cols] = product[block * 96 : (block + 1) * 96]
            outs[block][96:, cols] = taps


def product_blocks(place, contexts, grads, after):
    shape = jax.ShapeDtypeStruct((112, WIDTH), BF)
    vmem = pl.BlockSpec(memory_space=pltpu.VMEM)
    return pl.pallas_call(
        product_kernel,
        out_shape=(shape,) * 4,
        in_specs=[pl.BlockSpec(memory_space=pltpu.SMEM)]
        + [vmem] * (4 + len(grads))
        + [pl.BlockSpec(memory_space=pl.ANY)],
        out_specs=(vmem,) * 4,
        compiler_params=pltpu.CompilerParams(vmem_limit_bytes=VMEM),
        cost_estimate=pl.CostEstimate(flops=3 << 30, bytes_accessed=8 << 20, transcendentals=0),
        name="product_blocks",
    )(place, *contexts, *grads, after)


def combine_kernel(parts, sources, pieces, count, scale, *refs):
    ins, outs = refs[: parts * sources], refs[-1 - pieces : -1]
    held = refs[-1]
    start = 0
    for part in range(parts):
        group = ins[part * sources : (part + 1) * sources]
        total = group[0][...].astype(F32)
        for ref in group[1:]:
            total = total + ref[...].astype(F32)
        held[:, start : start + group[0].shape[1]] = total * scale
        start = start + group[0].shape[1]
    rows = count // pieces
    for piece in range(pieces):
        out = outs[piece]
        if out.shape[0] > rows + 16:
            out[...] = jnp.zeros_like(out)
        out[:rows] = held[piece * rows : (piece + 1) * rows].astype(out.dtype)
        out[rows : rows + 16] = held[count : count + 16].astype(out.dtype)


def combine(parts, count, pieces, out_rows, after):
    shape = jax.ShapeDtypeStruct((out_rows, WIDTH), BF)
    blocks = [block for part in parts for block in part]
    vmem = pl.BlockSpec(memory_space=pltpu.VMEM)
    return pl.pallas_call(
        functools.partial(combine_kernel, len(parts), len(parts[0]), pieces, count, 1.0),
        out_shape=(shape,) * pieces,
        in_specs=[vmem] * len(blocks) + [pl.BlockSpec(memory_space=pl.ANY)] * len(after),
        out_specs=(vmem,) * pieces,
        scratch_shapes=[pltpu.VMEM((blocks[0].shape[0], WIDTH), F32)],
        compiler_params=pltpu.CompilerParams(vmem_limit_bytes=VMEM),
        cost_estimate=pl.CostEstimate(flops=0, bytes_accessed=1024, transcendentals=0),
        name="combine",
    )(*blocks, *after)


def last_kernel(scale, *refs):
    ins, (weight_out, taps_out, held) = refs[:-3], refs[-3:]
    total = ins[0][...].astype(F32)
    for ref in ins[1:]:
        total = total + ref[...].astype(F32)
    held[...] = total * scale
    weight_out[...] = held[:6]
    taps_out[...] = held[6:22]


def last_combine(blocks, scale):
    return pl.pallas_call(
        functools.partial(last_kernel, scale),
        out_shape=(
            jax.ShapeDtypeStruct((6, WIDTH), F32),
            jax.ShapeDtypeStruct((16, WIDTH), F32),
        ),
        scratch_shapes=[pltpu.VMEM(blocks[0].shape, F32)],
        name="last_combine",
    )(*blocks)


def join_kernel(place_ref, mine, theirs, after, out, held):
    c = place_ref[3]
    held[pl.ds(pl.multiple_of(16 * c, 16), 16)] = mine[...]
    held[pl.ds(pl.multiple_of(16 * (1 - c), 16), 16)] = theirs[...]
    out[...] = held[:KW]


def join_taps(place, mine, theirs, after):
    vmem = pl.BlockSpec(memory_space=pltpu.VMEM)
    return pl.pallas_call(
        join_kernel,
        out_shape=jax.ShapeDtypeStruct((KW, WIDTH), F32),
        in_specs=[pl.BlockSpec(memory_space=pltpu.SMEM), vmem, vmem, pl.BlockSpec(memory_space=pl.ANY)],
        out_specs=vmem,
        scratch_shapes=[pltpu.VMEM((KW + 1, WIDTH), F32)],
        name="join_taps",
    )(place, mine, theirs, after)


def finish_kernel(*refs):
    dk, dv, later, earlier = refs[:4]
    for own, out, rows in ((dk, refs[-2], slice(0, ROWS)), (dv, refs[-1], slice(ROWS, 2 * ROWS))):
        total = own[...] + later[rows].astype(F32) + earlier[rows].astype(F32)
        out[...] = total.astype(BF)


def finish(operands):
    shape = jax.ShapeDtypeStruct((ROWS, WIDTH), BF)
    column = lambda rows: pl.BlockSpec((rows, CWIDTH), lambda i: (0, i))
    return pl.pallas_call(
        finish_kernel,
        grid=(CHUNKS,),
        out_shape=(shape, shape),
        in_specs=[column(ROWS), column(ROWS), column(2 * ROWS), column(2 * ROWS)],
        out_specs=(column(ROWS), column(ROWS)),
        compiler_params=pltpu.CompilerParams(vmem_limit_bytes=VMEM),
        cost_estimate=pl.CostEstimate(flops=0, bytes_accessed=1024, transcendentals=0),
        name="finish",
    )(*operands)


def seq_pairs(shift):
    pairs = []
    for source in range(64):
        z, x, c = source // 8, (source // 2) % 4, source % 2
        tz, tx, tc = shift(z, x, c)
        pairs.append((source, ((tz % 8) * 4 + tx % 4) * 2 + tc))
    return pairs


SWAP = seq_pairs(lambda z, x, c: (z, x, 1 - c))
PAIR = seq_pairs(lambda z, x, c: (z ^ 1, x, c))
BOTH = seq_pairs(lambda z, x, c: (z ^ 1, x, 1 - c))
UP = [(i, i + 1) for i in range(63)]
DOWN = [(i + 1, i) for i in range(63)]


def per_device(query, key, value, segments, out_proj, conv_kernel, cotangent):
    q, k, v, cot = query[0], key[0], value[0], cotangent[0]
    dp = lax.axis_index("dp")
    seq = lax.axis_index("seq")
    place = jnp.stack([dp, seq // 8, (seq // 2) % 4, seq % 2]).astype(jnp.int32)
    own_ids = segments[0] + 1

    id_row = lax.pad(
        own_ids.astype(BF)[None], jnp.zeros((), BF), ((0, 15, 0), (0, CWIDTH - ROWS, 0))
    )
    lows, highs = [], []
    for chunk in range(CHUNKS):
        cols = slice(chunk * CWIDTH, (chunk + 1) * CWIDTH)
        sent_up = [k[:, cols], v[:, cols], q[ROWS - EDGE :, cols], cot[ROWS - CEDGE :, cols], id_row]
        sent_down = [k[:, cols], v[:, cols], q[:EDGE, cols], cot[:CEDGE, cols], id_row]
        lows.append(lax.ppermute(jnp.concatenate(sent_up, axis=0), "seq", UP))
        highs.append(lax.ppermute(jnp.concatenate(sent_down, axis=0), "seq", DOWN))
    ids_now = own_ids.astype(F32)[None]
    taps = lax.pad(conv_kernel.astype(F32), jnp.zeros((), F32), ((0, 1, 0), (0, 0, 0)))

    attended = [
        attention_forward(
            ids_now, q, k, v, lows[chunk], highs[chunk], chunk
        )
        for chunk in range(CHUNKS)
    ]
    contexts = [entry[1] for entry in attended]
    row_ids = attended[0][3]
    ordered = order_context(place, contexts)
    ordered = [ordered[0]] + [
        lax.ppermute(part, "seq", pairs) for part, pairs in zip(ordered[1:], (SWAP, PAIR, BOTH))
    ]

    block_out, after = None, []
    grads, gathered = [], []
    relayed = None
    for call in range(len(CALLS)):
        block_out, grad = conv_chain(
            row_ids, contexts, out_proj, taps, lows, cot, highs, block_out, after, call
        )
        grads.append(grad)
        across = lax.ppermute(grad, "seq", PAIR)
        if call == 0:
            diagonal = lax.ppermute(across, "seq", SWAP)
        elif call == 1:
            relayed, diagonal = across, None
        else:
            diagonal = lax.ppermute(grad, "seq", BOTH)
            relayed, _ = lax.optimization_barrier((relayed, grad))
            gathered[7] = lax.ppermute(relayed, "seq", SWAP)
        group = [grad, lax.ppermute(grad, "seq", SWAP), across, diagonal]
        after = ordered[1:] if call == 0 else gathered[1:3]
        gathered += group
    context_grad = context_gradient(out_proj, grads, [gathered[3]])
    blocks = product_blocks(place, ordered, gathered, context_grad)
    got = [lax.ppermute(blocks[n], "dp", [(i, (i + n) % 4) for i in range(4)]) for n in (1, 2, 3)]

    results, after = (), [blocks[0]]
    for turn, (chunk, piece) in enumerate(((0, (0, 3)), (1, (0, 1)), (1, (1, 2)))):
        results = attention_backward(
            q, k, v, lows[chunk], highs[chunk], context_grad, attended[chunk][0],
            attended[chunk][2], results, after, chunk, piece,
        )
        if turn == 1:
            held = combine([[blocks[0]] + got], 96, 4, 40, [results[2]])
            after = [held[0]]
            got = [
                lax.ppermute(held[n], "seq", seq_pairs(lambda z, x, c: (z, x + n, c)))
                for n in (1, 2, 3)
            ]
    dq, low, dk, dv, high = results
    low, high, *got = lax.optimization_barrier((low, high, *got))
    later, earlier = lax.ppermute(low, "seq", DOWN), lax.ppermute(high, "seq", UP)
    held = combine([[held[0]] + got], 24, 4, 24, [dk])
    got = [
        lax.ppermute(held[n], "seq", seq_pairs(lambda z, x, c: (z + 2 * n, x, c))) for n in (1, 2, 3)
    ]
    scale_out = (4 * 64 * ROWS) ** (-0.5)
    grad_out_proj, taps_rows = last_combine([held[0]] + got, scale_out)
    taps_theirs = lax.ppermute(taps_rows, "seq", SWAP)
    dk, dv = finish([dk, dv, later, earlier])
    grad_kernel = join_taps(place, taps_rows, taps_theirs, dk)
    return (block_out[None], dq[None], dk[None], dv[None], grad_kernel, grad_out_proj)


def solution(mesh):
    in_specs = (
        P("dp", "seq", None),
        P("dp", "seq", None),
        P("dp", "seq", None),
        P("dp", "seq"),
        P(),
        P(),
        P("dp", "seq", None),
    )
    out_specs = (
        P("dp", "seq", None),
        P("dp", "seq", None),
        P("dp", "seq", None),
        P("dp", "seq", None),
        P(),
        P(("dp", "seq"), None),
    )
    return jax.shard_map(
        per_device, mesh=mesh, in_specs=in_specs, out_specs=out_specs, check_vma=False
    )
```

```python
import functools

import jax
import jax.numpy as jnp
from jax import lax
from jax.experimental import pallas as pl
from jax.experimental.pallas import tpu as pltpu
from jax.sharding import PartitionSpec as P

HD = 64
KW = 31
ROWS = 256
EDGE = 32
CEDGE = 16
QROWS = ROWS + 2 * EDGE
CROWS = ROWS + 2 * CEDGE
WINDOW = 3 * ROWS
WIDTH = 1536
CALLS = ((0, 3), (3, 2), (5, 1))
CHUNKS = 2
CWIDTH = WIDTH // CHUNKS
LANES = 256
VMEM = 60 * 1024 * 1024
BF = jnp.bfloat16
F32 = jnp.float32
NT = (((1,), (1,)), ((), ()))
TN = (((0,), (0,)), ((), ()))


def half_masks(scale):
    lane = lax.broadcasted_iota(jnp.int32, (1, 2 * HD), 1)
    return [
        jnp.where((lane < HD) == (half == 0), scale, 0.0).astype(BF) for half in range(2)
    ]


def pack_kernel(ids, k, v, q_first, q_last, cot_first, cot_last, up, down):
    for out, q_edge, cot_edge in ((up, q_last, cot_last), (down, q_first, cot_first)):
        out[:ROWS] = k[...]
        out[ROWS : 2 * ROWS] = v[...]
        out[2 * ROWS : 2 * ROWS + EDGE] = q_edge[...]
        out[2 * ROWS + EDGE : 2 * ROWS + EDGE + CEDGE] = cot_edge[...]
        out[2 * ROWS + EDGE + CEDGE :] = jnp.broadcast_to(ids[...], (16, ROWS)).astype(BF)


def pack_halo(ids, q, k, v, cot, chunk):
    first = chunk * (CWIDTH // ROWS)
    block = lambda rows, at=0: pl.BlockSpec((rows, ROWS), lambda i: (at, i + first))
    rows = 2 * ROWS + EDGE + CEDGE + 16
    shape = jax.ShapeDtypeStruct((rows, CWIDTH), BF)
    column = pl.BlockSpec((rows, ROWS), lambda i: (0, i))
    return pl.pallas_call(
        pack_kernel,
        grid=(CWIDTH // ROWS,),
        out_shape=(shape, shape),
        in_specs=[
            pl.BlockSpec((1, ROWS), lambda i: (0, 0)), block(ROWS), block(ROWS),
            block(EDGE), block(EDGE, ROWS // EDGE - 1),
            block(CEDGE), block(CEDGE, ROWS // CEDGE - 1),
        ],
        out_specs=(column, column),
        compiler_params=pltpu.CompilerParams(vmem_limit_bytes=VMEM),
        cost_estimate=pl.CostEstimate(flops=0, bytes_accessed=1024, transcendentals=0),
        name="pack_halo",
    )(ids, k, v, q, q, cot, cot)


def forward_kernel(
    ids_low, ids_own, ids_high, q_low, q_own, q_high, k_low, k_own, k_high, v_low, v_own, v_high,
    context_ref, context_b_ref, probs_ref, row_ids_ref, bias, turned,
):
    @pl.when(pl.program_id(0) == 0)
    def _():
        key_ids = jnp.concatenate(
            [ids_low[...].astype(F32)[:1], ids_own[...], ids_high[...].astype(F32)[:1]], axis=1
        )
        turned[...] = jnp.broadcast_to(key_ids, (128, WINDOW)).T
        row_ids = turned[ROWS - EDGE : 2 * ROWS + EDGE]
        row_ids_ref[...] = row_ids
        bias[...] = jnp.where(row_ids[:, :1] == key_ids, 0.0, -1e30)

    scales = half_masks(HD ** -0.5)
    lane = lax.broadcasted_iota(jnp.int32, (1, 2 * HD), 1) < HD
    for pair in range(q_own.shape[1] // (2 * HD)):
        cols = slice(pair * 2 * HD, (pair + 1) * 2 * HD)
        q = jnp.concatenate([q_low[:, cols], q_own[:, cols], q_high[:, cols]], axis=0)
        k = jnp.concatenate([k_low[:, cols], k_own[:, cols], k_high[:, cols]], axis=0)
        v = jnp.concatenate([v_low[:, cols], v_own[:, cols], v_high[:, cols]], axis=0)
        outs = []
        for half in range(2):
            scores = lax.dot_general(q * scales[half], k, NT, preferred_element_type=F32)
            scores = scores + bias[...]
            highest = jnp.max(scores, axis=1, keepdims=True)
            weights = jnp.exp(scores - highest)
            totals = jnp.sum(weights, axis=1, keepdims=True)
            probs = (weights * (1.0 / totals)).astype(BF)
            probs_ref[2 * pair + half] = probs[EDGE : EDGE + ROWS]
            outs.append(jnp.dot(probs, v, preferred_element_type=F32))
        context = jnp.where(lane, outs[0], outs[1])
        context_ref[:, cols] = context[EDGE : EDGE + ROWS]
        context_b_ref[:, cols] = context.astype(BF)


def attention_forward(own_ids, q, k, v, low, high, chunk):
    step = 4 * HD
    heads = step // HD
    first = chunk * (CWIDTH // step)
    column = lambda rows: pl.BlockSpec((rows, step), lambda i: (0, i))
    offset = lambda rows, at=0: pl.BlockSpec((rows, step), lambda i: (at, i + first))
    second = pl.BlockSpec((ROWS, step), lambda i: (1, i))
    edge = pl.BlockSpec((EDGE, step), lambda i: (2 * ROWS // EDGE, i))
    whole = lambda shape: pl.BlockSpec(shape, lambda i: (0, 0))
    id_block = pl.BlockSpec((16, ROWS), lambda i: ((2 * ROWS + EDGE + CEDGE) // 16, 0))
    return pl.pallas_call(
        forward_kernel,
        grid=(CWIDTH // step,),
        out_shape=(
            jax.ShapeDtypeStruct((ROWS, CWIDTH), F32),
            jax.ShapeDtypeStruct((QROWS, CWIDTH), BF),
            jax.ShapeDtypeStruct((CWIDTH // HD, ROWS, WINDOW), BF),
            jax.ShapeDtypeStruct((QROWS, 128), F32),
        ),
        in_specs=[
            id_block, whole((1, ROWS)), id_block, edge, offset(ROWS), edge,
            column(ROWS), offset(ROWS), column(ROWS), second, offset(ROWS), second,
        ],
        out_specs=(
            column(ROWS),
            column(QROWS),
            pl.BlockSpec((heads, ROWS, WINDOW), lambda i: (i, 0, 0)),
            whole((QROWS, 128)),
        ),
        scratch_shapes=[pltpu.VMEM((QROWS, WINDOW), F32), pltpu.VMEM((WINDOW, 128), F32)],
        compiler_params=pltpu.CompilerParams(vmem_limit_bytes=VMEM),
        cost_estimate=pl.CostEstimate(
            flops=12 << 30, bytes_accessed=10 << 20, transcendentals=0
        ),
        name="attention_forward",
    )(low, own_ids, high, low, q, high, low, k, high, low, v, high)


def conv_kernel_body(*refs):
    ids_ref = refs[0]
    contexts = refs[1 : 1 + CHUNKS]
    weight_ref, taps_ref, cot_low, cot_own, cot_high = refs[1 + CHUNKS : 6 + CHUNKS]
    rest = refs[6 + CHUNKS :]
    block_ref, grad_ref, shifted, cgrad, ids, gated, taps_acc, cot_ref = rest[-8:]
    step = pl.program_id(0)

    @pl.when(step == 0)
    def _():
        ids[0] = ids_ref[...]
        for b in range(1, 8):
            ids[b, : QROWS - 8] = ids_ref[b : b + QROWS - 8, :]

    cot_ref[:CEDGE] = cot_low[...].astype(F32)
    cot_ref[CEDGE : CEDGE + ROWS] = cot_own[...].astype(F32)
    cot_ref[CEDGE + ROWS :] = cot_high[...].astype(F32)
    attended = jnp.zeros((QROWS, LANES), F32)
    for n, context_ref in enumerate(contexts):
        attended = attended + jnp.dot(
            context_ref[...], weight_ref[n * CWIDTH : (n + 1) * CWIDTH], preferred_element_type=F32
        )
    shifted[0] = attended.astype(BF).astype(F32)
    for b in range(1, 8):
        shifted[b, : QROWS - 8] = shifted[0, b : b + QROWS - 8, :]
    taps_acc[...] = jnp.zeros_like(taps_acc)
    tiles = [slice(j * 128, (j + 1) * 128) for j in range(LANES // 128)]
    block = 32

    def forward_rows(i, carry):
        o = pl.multiple_of(i * block, block)
        own = ids[0, pl.ds(o + CEDGE, block), :]
        sums = [jnp.zeros((block, 128), F32) for _ in tiles]
        for e in range(1, KW + 1):
            a, b = divmod(e, 8)
            same = ids[b, pl.ds(o + 8 * a, block), :] == own
            for j, tile in enumerate(tiles):
                term = shifted[b, pl.ds(o + 8 * a, block), tile] * taps_ref[e - 1 : e, tile]
                sums[j] = sums[j] + jnp.where(same, term, 0.0)
        for j, tile in enumerate(tiles):
            gate = jax.nn.sigmoid(sums[j])
            gated[pl.ds(o, block), tile] = sums[j] * gate
            grad = cot_ref[pl.ds(o, block), tile] * gate * (1.0 + sums[j] * (1.0 - gate))
            cgrad[0, pl.ds(o, block), tile] = grad.astype(BF).astype(F32)
        return carry

    lax.fori_loop(0, CROWS // block, forward_rows, 0)
    block_ref[...] = gated[CEDGE : CEDGE + ROWS].astype(BF)
    for b in range(1, 8):
        cgrad[b, : CROWS - 8] = cgrad[0, b : b + CROWS - 8, :]

    def backward_rows(i, carry):
        s = pl.multiple_of(i * block, block)
        own = ids[0, pl.ds(s + EDGE, block), :]
        grads = [cgrad[0, pl.ds(s + CEDGE, block), tile] for tile in tiles]
        sums = [jnp.zeros((block, 128), F32) for _ in tiles]
        for e in range(1, KW + 1):
            a, b = divmod(e, 8)
            same = ids[b, pl.ds(s + CEDGE + 8 * a, block), :] == own
            for j, tile in enumerate(tiles):
                term = cgrad[b, pl.ds(s + 8 * a, block), tile] * taps_ref[KW - e : KW - e + 1, tile]
                sums[j] = sums[j] + jnp.where(same, term, 0.0)
                pair = grads[j] * shifted[b, pl.ds(s + CEDGE + 8 * a, block), tile]
                pair = jnp.where(same, pair, 0.0)
                taps_acc[e - 1, :, tile] += jnp.sum(pair.reshape(block // 8, 8, 128), axis=0)
        for j, tile in enumerate(tiles):
            grad_ref[pl.ds(s, block), tile] = sums[j].astype(BF)
        return carry

    lax.fori_loop(0, ROWS // block, backward_rows, 0)
    grad_ref[ROWS:] = jnp.sum(taps_acc[...], axis=1).astype(BF)


def conv_chain(row_ids, contexts, out_proj, taps, lows, cot, highs, block_out, after, call):
    begin, steps = CALLS[call]
    first = call == 0
    width = steps * LANES
    column = lambda rows: pl.BlockSpec((rows, LANES), lambda i: (0, i))
    offset = lambda rows, at=0: pl.BlockSpec((rows, LANES), lambda i: (at, i + begin))
    whole = lambda shape: pl.BlockSpec(shape, lambda i: (0, 0))
    anywhere = pl.BlockSpec(memory_space=pl.ANY)
    chunk = begin * LANES // CWIDTH
    local = begin - chunk * (CWIDTH // LANES)
    edge = pl.BlockSpec((CEDGE, LANES), lambda i: ((2 * ROWS + EDGE) // CEDGE, i + local))
    carried = after if first else [block_out] + after
    return pl.pallas_call(
        conv_kernel_body,
        grid=(steps,),
        out_shape=(
            jax.ShapeDtypeStruct((ROWS, WIDTH), BF),
            jax.ShapeDtypeStruct((ROWS + KW + 1, width), BF),
        ),
        in_specs=[whole((QROWS, 128))]
        + [whole((QROWS, CWIDTH))] * CHUNKS
        + [
            offset(WIDTH), offset(KW + 1),
            edge, offset(ROWS), edge,
        ]
        + [anywhere] * len(carried),
        out_specs=(offset(ROWS), column(ROWS + KW + 1)),
        scratch_shapes=[
            pltpu.VMEM((8, QROWS, LANES), F32),
            pltpu.VMEM((8, CROWS, LANES), F32),
            pltpu.VMEM((8, QROWS, 128), F32),
            pltpu.VMEM((CROWS, LANES), F32),
            pltpu.VMEM((KW + 1, 8, LANES), F32),
            pltpu.VMEM((CROWS, LANES), F32),
        ],
        input_output_aliases={} if first else {6 + CHUNKS: 0},
        compiler_params=pltpu.CompilerParams(vmem_limit_bytes=VMEM),
        cost_estimate=pl.CostEstimate(
            flops=steps * (5 << 30), bytes_accessed=10 << 20, transcendentals=0
        ),
        name="conv_chain",
    )(row_ids, *contexts, out_proj, taps, lows[chunk], cot, highs[chunk], *carried)


def context_grad_kernel(weight_ref, *refs):
    grads, out = refs[: len(CALLS)], refs[-1]
    total = jnp.zeros(out.shape[::-1], F32)
    for (begin, steps), grad in zip(CALLS, grads):
        cols = slice(begin * LANES, (begin + steps) * LANES)
        total = total + lax.dot_general(
            weight_ref[:, cols], grad[:ROWS], NT, preferred_element_type=F32
        )
    out[...] = total.T.astype(BF)


def context_gradient(out_proj, grads, after):
    step = 768
    return pl.pallas_call(
        context_grad_kernel,
        grid=(WIDTH // step,),
        out_shape=jax.ShapeDtypeStruct((ROWS, WIDTH), BF),
        in_specs=[pl.BlockSpec((step, WIDTH), lambda i: (i, 0))]
        + [pl.BlockSpec(grad.shape, lambda i: (0, 0)) for grad in grads]
        + [pl.BlockSpec(memory_space=pl.ANY)] * len(after),
        out_specs=pl.BlockSpec((ROWS, step), lambda i: (0, i)),
        compiler_params=pltpu.CompilerParams(vmem_limit_bytes=VMEM),
        cost_estimate=pl.CostEstimate(flops=3 << 30, bytes_accessed=8 << 20, transcendentals=0),
        name="context_gradient",
    )(out_proj, *grads, *after)


def backward_kernel(
    q_own, k_low, k_own, k_high, v_low, v_own, v_high, upstream, context, probs_ref, *rest,
):
    dq_ref, low_ref, dk_own, dv_own, high_ref = rest[-5:]
    plain = half_masks(1.0)
    scales = half_masks(HD ** -0.5)
    lane = lax.broadcasted_iota(jnp.int32, (1, 2 * HD), 1) < HD
    for pair in range(q_own.shape[1] // (2 * HD)):
        cols = slice(pair * 2 * HD, (pair + 1) * 2 * HD)
        k = jnp.concatenate([k_low[:, cols], k_own[:, cols], k_high[:, cols]], axis=0)
        v = jnp.concatenate([v_low[:, cols], v_own[:, cols], v_high[:, cols]], axis=0)
        q = q_own[:, cols]
        up = upstream[:, cols]
        products = up.astype(F32) * context[:, cols]
        q_turned = q.astype(F32).T.astype(BF)
        up_turned = up.astype(F32).T.astype(BF)
        dqs, dks, dvs = [], [], []
        for half in range(2):
            rows = slice(half * HD, (half + 1) * HD)
            delta = jnp.sum(
                jnp.where(lane == (half == 0), products, 0.0), axis=1, keepdims=True
            ) * HD ** -0.5
            grads = lax.dot_general(up * scales[half], v, NT, preferred_element_type=F32)
            probs = probs_ref[2 * pair + half]
            score_grad = (probs.astype(F32) * (grads - delta)).astype(BF)
            dqs.append(jnp.dot(score_grad, k, preferred_element_type=F32))
            dks.append(jnp.dot(q_turned[rows], score_grad, preferred_element_type=F32))
            dvs.append(jnp.dot(up_turned[rows], probs, preferred_element_type=F32))
        dq_ref[:, cols] = jnp.where(lane, dqs[0], dqs[1]).astype(BF)
        for n, (parts, own) in enumerate(((dks, dk_own), (dvs, dv_own))):
            whole = jnp.concatenate(parts, axis=0).T
            low_ref[n * ROWS : (n + 1) * ROWS, cols] = whole[:ROWS].astype(BF)
            own[:, cols] = whole[ROWS : 2 * ROWS]
            high_ref[n * ROWS : (n + 1) * ROWS, cols] = whole[2 * ROWS :].astype(BF)


def attention_backward(q, k, v, low, high, upstream, context, probs, previous, after, chunk, piece):
    step = 4 * HD
    heads = step // HD
    inner, count = piece
    first = chunk * (CWIDTH // step) + inner
    column = lambda rows: pl.BlockSpec((rows, step), lambda i: (0, i + inner))
    offset = lambda rows: pl.BlockSpec((rows, step), lambda i: (0, i + first))
    second = pl.BlockSpec((ROWS, step), lambda i: (1, i + inner))
    own = jax.ShapeDtypeStruct((ROWS, WIDTH), F32)
    both = jax.ShapeDtypeStruct((2 * ROWS, WIDTH), BF)
    carried = list(previous) + after
    return pl.pallas_call(
        backward_kernel,
        grid=(count,),
        out_shape=(jax.ShapeDtypeStruct((ROWS, WIDTH), BF), both, own, own, both),
        in_specs=[
            offset(ROWS), column(ROWS), offset(ROWS), column(ROWS), second, offset(ROWS), second,
            offset(ROWS), column(ROWS),
            pl.BlockSpec((heads, ROWS, WINDOW), lambda i: (i + inner, 0, 0)),
        ]
        + [pl.BlockSpec(memory_space=pl.ANY)] * len(carried),
        out_specs=(
            offset(ROWS), offset(2 * ROWS), offset(ROWS), offset(ROWS), offset(2 * ROWS),
        ),
        input_output_aliases={10 + n: n for n in range(len(previous))},
        compiler_params=pltpu.CompilerParams(vmem_limit_bytes=VMEM),
        cost_estimate=pl.CostEstimate(
            flops=count * (3 << 30), bytes_accessed=10 << 20, transcendentals=0
        ),
        name="attention_backward",
    )(q, low, k, high, low, v, high, upstream, context, probs, *carried)


def order_kernel(place_ref, *refs):
    contexts, outs = refs[:CHUNKS], refs[CHUNKS:]
    dp, z, x, c = (place_ref[n] for n in range(4))
    span = WIDTH // 4
    row = lax.broadcasted_iota(jnp.int32, (span, 1), 0)
    quarter = row // 96
    tc = lax.rem(quarter + c, 2)
    tl = lax.rem(quarter // 2 + z, 2)
    tx = lax.rem(lax.rem(row, 96) // 24 + x, 4)
    th = lax.rem(lax.rem(row, 24) // 6 + z // 2, 4)
    target = 48 * (2 * th + tl) + 12 * tx + 6 * tc + lax.rem(row, 6)
    chosen = jnp.where(
        target == lax.broadcasted_iota(jnp.int32, (1, span), 1), 1.0, 0.0
    ).astype(BF)
    turned = []
    for ref in contexts:
        for n in range(CWIDTH // span):
            part = ref[EDGE : EDGE + ROWS, n * span : (n + 1) * span]
            turned.append(lax.dot_general(chosen, part, NT, preferred_element_type=F32).astype(BF))
    for n in range(4):
        at = pl.ds(pl.multiple_of(96 * lax.rem(n - dp + 4, 4), 32), 96)
        for index, out in enumerate(outs):
            out[at] = turned[n][96 * index : 96 * (index + 1)]


def order_context(place, contexts):
    shape = jax.ShapeDtypeStruct((WIDTH // 4, ROWS), BF)
    vmem = pl.BlockSpec(memory_space=pltpu.VMEM)
    return pl.pallas_call(
        order_kernel,
        out_shape=(shape,) * 4,
        in_specs=[pl.BlockSpec(memory_space=pltpu.SMEM)] + [vmem] * CHUNKS,
        out_specs=(vmem,) * 4,
        compiler_params=pltpu.CompilerParams(vmem_limit_bytes=VMEM),
        name="order_context",
    )(place, *contexts)


def product_kernel(place_ref, *refs):
    contexts, grads, outs = refs[:4], refs[4:-5], refs[-4:]
    at = pl.ds(pl.multiple_of(ROWS + 16 * place_ref[3], 16), 16)
    context = jnp.concatenate([ref[...] for ref in contexts], axis=1)
    for call, (begin, steps) in enumerate(CALLS):
        cols = slice(begin * LANES, (begin + steps) * LANES)
        group = grads[4 * call : 4 * call + 4]
        taps = sum(grad[at].astype(F32) for grad in group).astype(BF)
        grad = jnp.concatenate([ref[:ROWS] for ref in group], axis=0)
        product = jnp.dot(context, grad, preferred_element_type=F32).astype(BF)
        for block in range(4):
            outs[block][:96, cols] = product[block * 96 : (block + 1) * 96]
            outs[block][96:, cols] = taps


def product_blocks(place, contexts, grads, after):
    shape = jax.ShapeDtypeStruct((112, WIDTH), BF)
    vmem = pl.BlockSpec(memory_space=pltpu.VMEM)
    return pl.pallas_call(
        product_kernel,
        out_shape=(shape,) * 4,
        in_specs=[pl.BlockSpec(memory_space=pltpu.SMEM)]
        + [vmem] * (4 + len(grads))
        + [pl.BlockSpec(memory_space=pl.ANY)],
        out_specs=(vmem,) * 4,
        compiler_params=pltpu.CompilerParams(vmem_limit_bytes=VMEM),
        cost_estimate=pl.CostEstimate(flops=3 << 30, bytes_accessed=8 << 20, transcendentals=0),
        name="product_blocks",
    )(place, *contexts, *grads, after)


def combine_kernel(parts, sources, pieces, count, scale, *refs):
    ins, outs = refs[: parts * sources], refs[-1 - pieces : -1]
    held = refs[-1]
    start = 0
    for part in range(parts):
        group = ins[part * sources : (part + 1) * sources]
        total = group[0][...].astype(F32)
        for ref in group[1:]:
            total = total + ref[...].astype(F32)
        held[:, start : start + group[0].shape[1]] = total * scale
        start = start + group[0].shape[1]
    rows = count // pieces
    for piece in range(pieces):
        out = outs[piece]
        if out.shape[0] > rows + 16:
            out[...] = jnp.zeros_like(out)
        out[:rows] = held[piece * rows : (piece + 1) * rows].astype(out.dtype)
        out[rows : rows + 16] = held[count : count + 16].astype(out.dtype)


def combine(parts, count, pieces, out_rows, after):
    shape = jax.ShapeDtypeStruct((out_rows, WIDTH), BF)
    blocks = [block for part in parts for block in part]
    vmem = pl.BlockSpec(memory_space=pltpu.VMEM)
    return pl.pallas_call(
        functools.partial(combine_kernel, len(parts), len(parts[0]), pieces, count, 1.0),
        out_shape=(shape,) * pieces,
        in_specs=[vmem] * len(blocks) + [pl.BlockSpec(memory_space=pl.ANY)] * len(after),
        out_specs=(vmem,) * pieces,
        scratch_shapes=[pltpu.VMEM((blocks[0].shape[0], WIDTH), F32)],
        compiler_params=pltpu.CompilerParams(vmem_limit_bytes=VMEM),
        cost_estimate=pl.CostEstimate(flops=0, bytes_accessed=1024, transcendentals=0),
        name="combine",
    )(*blocks, *after)


def last_kernel(scale, *refs):
    ins, (weight_out, taps_out, held) = refs[:-3], refs[-3:]
    total = ins[0][...].astype(F32)
    for ref in ins[1:]:
        total = total + ref[...].astype(F32)
    held[...] = total * scale
    weight_out[...] = held[:6]
    taps_out[...] = held[6:22]


def last_combine(blocks, scale):
    return pl.pallas_call(
        functools.partial(last_kernel, scale),
        out_shape=(
            jax.ShapeDtypeStruct((6, WIDTH), F32),
            jax.ShapeDtypeStruct((16, WIDTH), F32),
        ),
        scratch_shapes=[pltpu.VMEM(blocks[0].shape, F32)],
        name="last_combine",
    )(*blocks)


def join_kernel(place_ref, mine, theirs, after, out, held):
    c = place_ref[3]
    held[pl.ds(pl.multiple_of(16 * c, 16), 16)] = mine[...]
    held[pl.ds(pl.multiple_of(16 * (1 - c), 16), 16)] = theirs[...]
    out[...] = held[:KW]


def join_taps(place, mine, theirs, after):
    vmem = pl.BlockSpec(memory_space=pltpu.VMEM)
    return pl.pallas_call(
        join_kernel,
        out_shape=jax.ShapeDtypeStruct((KW, WIDTH), F32),
        in_specs=[pl.BlockSpec(memory_space=pltpu.SMEM), vmem, vmem, pl.BlockSpec(memory_space=pl.ANY)],
        out_specs=vmem,
        scratch_shapes=[pltpu.VMEM((KW + 1, WIDTH), F32)],
        name="join_taps",
    )(place, mine, theirs, after)


def finish_kernel(*refs):
    dk, dv, later, earlier = refs[:4]
    for own, out, rows in ((dk, refs[-2], slice(0, ROWS)), (dv, refs[-1], slice(ROWS, 2 * ROWS))):
        total = own[...] + later[rows].astype(F32) + earlier[rows].astype(F32)
        out[...] = total.astype(BF)


def finish(operands):
    shape = jax.ShapeDtypeStruct((ROWS, WIDTH), BF)
    column = lambda rows: pl.BlockSpec((rows, CWIDTH), lambda i: (0, i))
    return pl.pallas_call(
        finish_kernel,
        grid=(CHUNKS,),
        out_shape=(shape, shape),
        in_specs=[column(ROWS), column(ROWS), column(2 * ROWS), column(2 * ROWS)],
        out_specs=(column(ROWS), column(ROWS)),
        compiler_params=pltpu.CompilerParams(vmem_limit_bytes=VMEM),
        cost_estimate=pl.CostEstimate(flops=0, bytes_accessed=1024, transcendentals=0),
        name="finish",
    )(*operands)


def seq_pairs(shift):
    pairs = []
    for source in range(64):
        z, x, c = source // 8, (source // 2) % 4, source % 2
        tz, tx, tc = shift(z, x, c)
        pairs.append((source, ((tz % 8) * 4 + tx % 4) * 2 + tc))
    return pairs


SWAP = seq_pairs(lambda z, x, c: (z, x, 1 - c))
PAIR = seq_pairs(lambda z, x, c: (z ^ 1, x, c))
BOTH = seq_pairs(lambda z, x, c: (z ^ 1, x, 1 - c))
UP = [(i, i + 1) for i in range(63)]
DOWN = [(i + 1, i) for i in range(63)]


def per_device(query, key, value, segments, out_proj, conv_kernel, cotangent):
    q, k, v, cot = query[0], key[0], value[0], cotangent[0]
    dp = lax.axis_index("dp")
    seq = lax.axis_index("seq")
    place = jnp.stack([dp, seq // 8, (seq // 2) % 4, seq % 2]).astype(jnp.int32)
    own_ids = segments[0] + 1

    ids_now = own_ids.astype(F32)[None]
    lows, highs = [], []
    for chunk in range(CHUNKS):
        sent_up, sent_down = pack_halo(ids_now, q, k, v, cot, chunk)
        lows.append(lax.ppermute(sent_up, "seq", UP))
        highs.append(lax.ppermute(sent_down, "seq", DOWN))
    taps = lax.pad(conv_kernel.astype(F32), jnp.zeros((), F32), ((0, 1, 0), (0, 0, 0)))

    attended = [
        attention_forward(
            ids_now, q, k, v, lows[chunk], highs[chunk], chunk
        )
        for chunk in range(CHUNKS)
    ]
    contexts = [entry[1] for entry in attended]
    row_ids = attended[0][3]
    ordered = order_context(place, contexts)
    ordered = [ordered[0]] + [
        lax.ppermute(part, "seq", pairs) for part, pairs in zip(ordered[1:], (SWAP, PAIR, BOTH))
    ]

    block_out, after = None, []
    grads, gathered = [], []
    relayed = None
    for call in range(len(CALLS)):
        block_out, grad = conv_chain(
            row_ids, contexts, out_proj, taps, lows, cot, highs, block_out, after, call
        )
        grads.append(grad)
        across = lax.ppermute(grad, "seq", PAIR)
        if call == 0:
            diagonal = lax.ppermute(across, "seq", SWAP)
        elif call == 1:
            relayed, diagonal = across, None
        else:
            diagonal = lax.ppermute(grad, "seq", BOTH)
            relayed, _ = lax.optimization_barrier((relayed, grad))
            gathered[7] = lax.ppermute(relayed, "seq", SWAP)
        group = [grad, lax.ppermute(grad, "seq", SWAP), across, diagonal]
        after = ordered[1:] if call == 0 else gathered[1:3]
        gathered += group
    context_grad = context_gradient(out_proj, grads, [gathered[3]])
    blocks = product_blocks(place, ordered, gathered, context_grad)
    got = [lax.ppermute(blocks[n], "dp", [(i, (i + n) % 4) for i in range(4)]) for n in (1, 2, 3)]

    results, after = (), [blocks[0]]
    for turn, (chunk, piece) in enumerate(((0, (0, 3)), (1, (0, 1)), (1, (1, 2)))):
        results = attention_backward(
            q, k, v, lows[chunk], highs[chunk], context_grad, attended[chunk][0],
            attended[chunk][2], results, after, chunk, piece,
        )
        if turn == 1:
            held = combine([[blocks[0]] + got], 96, 4, 40, [results[2]])
            after = [held[0]]
            got = [
                lax.ppermute(held[n], "seq", seq_pairs(lambda z, x, c: (z, x + n, c)))
                for n in (1, 2, 3)
            ]
    dq, low, dk, dv, high = results
    low, high, *got = lax.optimization_barrier((low, high, *got))
    later, earlier = lax.ppermute(low, "seq", DOWN), lax.ppermute(high, "seq", UP)
    held = combine([[held[0]] + got], 24, 4, 24, [dk])
    got = [
        lax.ppermute(held[n], "seq", seq_pairs(lambda z, x, c: (z + 2 * n, x, c))) for n in (1, 2, 3)
    ]
    scale_out = (4 * 64 * ROWS) ** (-0.5)
    grad_out_proj, taps_rows = last_combine([held[0]] + got, scale_out)
    taps_theirs = lax.ppermute(taps_rows, "seq", SWAP)
    dk, dv = finish([dk, dv, later, earlier])
    grad_kernel = join_taps(place, taps_rows, taps_theirs, dk)
    return (block_out[None], dq[None], dk[None], dv[None], grad_kernel, grad_out_proj)


def solution(mesh):
    in_specs = (
        P("dp", "seq", None),
        P("dp", "seq", None),
        P("dp", "seq", None),
        P("dp", "seq"),
        P(),
        P(),
        P("dp", "seq", None),
    )
    out_specs = (
        P("dp", "seq", None),
        P("dp", "seq", None),
        P("dp", "seq", None),
        P("dp", "seq", None),
        P(),
        P(("dp", "seq"), None),
    )
    return jax.shard_map(
        per_device, mesh=mesh, in_specs=in_specs, out_specs=out_specs, check_vma=False
    )
```
